256 devices in a mesh: queue: 128 (over y_hi, x, z, core), heads: 2 (over y_lo).
Axes of the slice: x: 4, y: 4 (y_hi: 2, y_lo: 2; y = y_hi * 2 + y_lo), z: 8, core: 2. Of those that a mesh axis runs over, the one named last changes fastest.
Arguments:
- latents: bfloat16 [128, 256, 1536], P('queue', None, 'heads'), may hold values from -6 to 6
- fresh_noise: bfloat16 [2, 256, 1536], P(None, None, 'heads'), may hold values from -6 to 6
- level_index: int32 [128], replicated, may hold values from 0 to 1023, as said below
- window_width: int32 [128], replicated, may hold values from 1 to 2
- w_mod: bfloat16 [256, 3, 1536], P(None, None, 'heads'), may hold values from -0.375 to 0.375
- w_query: bfloat16 [1536, 1536], P(None, 'heads'), may hold values from -1 to 1
- w_key: bfloat16 [1536, 1536], P(None, 'heads'), may hold values from -1 to 1
- w_value: bfloat16 [1536, 1536], P(None, 'heads'), may hold values from -0.15625 to 0.15625
- w_out: bfloat16 [1536, 1536], P('heads'), may hold values from -0.15625 to 0.15625
Outputs:
- queue_out: bfloat16 [128, 256, 1536], P('queue', None, 'heads')
- velocities: bfloat16 [2, 128, 256, 1536], P(None, 'queue', None, 'heads')
The draws below stay inside these ranges and needn't reach their ends.
Inputs may be any that keep to these rules, and one draw needn't show every extreme that they name: `level_index`: strictly rising along the queue: slot f holds a level in [f * 8, (f + 1) * 8); slot 0 holds 0 and the last slot 1023.
All inputs are finite; a program needn't handle non-finite values.
Results may differ from the reference program's by a relative error of at most 0.008.
Values may be sent and summed in bfloat16 or wider, within the bound.
No kernel may reach another device: no remote copies, remote signals or barrier semaphores. Data moves between devices by JAX's collectives and lax.ppermute only.
A program may use at most 64 MiB of HBM per device.

```python
import math
import jax
import jax.numpy as jnp
from jax import lax

D = 1536
HEADS = 12
HEAD_DIM = 128
FREQ = 256
ROWS = 256
HALO = 2
STRIDE = 8
STEPS = 2
FRAMES = 128
LEVELS = 1024


def draw_level_index(key, part):
    key = jax.random.fold_in(key, 11)
    offset = jax.random.randint(key, (FRAMES,), 0, STRIDE)
    offset = offset.at[0].set(0).at[FRAMES - 1].set(STRIDE - 1)
    return (jnp.arange(FRAMES, dtype=jnp.int32) * STRIDE + offset).astype(jnp.int32)


def draw_window_width(key, part):
    key = jax.random.fold_in(key, 12)
    widths = jax.random.randint(key, (FRAMES,), 1, HALO + 1)
    widths = widths.at[1].set(HALO).at[2].set(1)
    return widths.astype(jnp.int32)


def draw_w_query(key, part):
    key = jax.random.fold_in(key, 21)
    values = jax.random.normal(key, (D, D), jnp.float32) / math.sqrt(D)
    return jnp.clip(values, -1.0, 1.0).astype(jnp.bfloat16)


def draw_w_key(key, part):
    key = jax.random.fold_in(key, 23)
    values = jax.random.normal(key, (D, D), jnp.float32) / math.sqrt(D)
    return jnp.clip(values, -1.0, 1.0).astype(jnp.bfloat16)


def block_levels(stream_key, extent, cuts, least, high):
    def one(axis_at, blocks):
        steps = jax.random.uniform(jax.random.fold_in(jax.random.fold_in(stream_key, 6), axis_at), (blocks,), jnp.float32, least / len(cuts), high / len(cuts))
        return jnp.repeat(jnp.exp(steps), extent[axis_at] // blocks).reshape((-1,) + (1,) * (len(extent) - axis_at - 1))

    gain = one(*cuts[0])
    for cut in cuts[1:]:
        gain = gain * one(*cut)
    return gain


def normal_values(key, shape, spread, limit, pieces=(), kind=jnp.bfloat16):
    array = spread * jax.random.normal(key, shape, jnp.float32)
    if pieces:
        array = array * block_levels(key, shape, pieces, -0.22, 0.18)
    return jnp.clip(array, -limit, limit).astype(kind)


def setup_inputs(seed: int = 0) -> dict:
    key_of = jax.random.split(jax.random.key(seed), 10)
    return {
        "latents": normal_values(key_of[0], (FRAMES, ROWS, D), 1.0, 6.0, ((0, 128), (2, 2))),
        "fresh_noise": normal_values(key_of[1], (STEPS, ROWS, D), 1.0, 6.0, ((2, 2),)),
        "level_index": draw_level_index(jax.random.fold_in(key_of[9], 71), 0),
        "window_width": draw_window_width(jax.random.fold_in(key_of[9], 71), 0),
        "w_mod": normal_values(key_of[4], (FREQ, 3, D), FREQ ** -0.5, 0.375, ((2, 2),)),
        "w_query": draw_w_query(jax.random.fold_in(key_of[9], 71), 0),
        "w_key": draw_w_key(jax.random.fold_in(key_of[9], 71), 0),
        "w_value": normal_values(key_of[7], (D, D), D ** -0.5, 0.15625, ((1, 2),)),
        "w_out": normal_values(key_of[8], (D, D), D ** -0.5, 0.15625, ((0, 2),)),
    }


norm_eps = 1e-06

def sigma_of(level, levels):
    share = level.astype(jnp.float32) / levels
    return 5.0 * share / (1.0 + 4.0 * share)

def embed_levels(level, half_width):
    index_k = jnp.arange(half_width, dtype=jnp.float32)
    frequency = jnp.exp(-math.log(10000.0) * index_k / half_width)
    phase = level.astype(jnp.float32)[..., None] * frequency
    return jnp.concatenate([jnp.cos(phase), jnp.sin(phase)], axis=-1).astype(jnp.bfloat16)

def reference(latents, fresh_noise, level_index, window_width, w_mod, w_query, w_key, w_value, w_out):
    sigma_here = sigma_of(level_index, LEVELS)
    sigma_next = jnp.concatenate([jnp.zeros((1,), jnp.float32), sigma_here[:-1]])
    embedding = embed_levels(level_index, FREQ // 2)
    modulation = jnp.dot(embedding, w_mod.reshape(FREQ, 3 * D), preferred_element_type=jnp.float32).reshape(FRAMES, 3, D)
    shift_rows = modulation[:, 0][:, None, :]
    scale_rows = modulation[:, 1][:, None, :]
    gate_rows = modulation[:, 2][:, None, :]
    offsets = jnp.arange(-HALO, HALO + 1, dtype=jnp.int32)
    latent = latents
    outputs = []
    for step_index in range(STEPS):
        float_state = latent.astype(jnp.float32)
        row_mean = lax.optimization_barrier(jnp.mean(float_state, axis=-1, keepdims=True))
        mean_square = lax.optimization_barrier(jnp.mean(float_state * float_state, axis=-1, keepdims=True))
        variance = mean_square - row_mean * row_mean
        normed = ((float_state - row_mean) * lax.rsqrt(variance + norm_eps) * (1.0 + scale_rows) + shift_rows).astype(jnp.bfloat16)
        flat = normed.reshape(FRAMES * ROWS, D)
        queries = jnp.dot(flat, w_query, preferred_element_type=jnp.float32).astype(jnp.bfloat16).reshape(FRAMES, ROWS, HEADS, HEAD_DIM)
        keys_all = jnp.dot(flat, w_key, preferred_element_type=jnp.float32).astype(jnp.bfloat16).reshape(FRAMES, ROWS, HEADS, HEAD_DIM)
        values_all = jnp.dot(flat, w_value, preferred_element_type=jnp.float32).astype(jnp.bfloat16).reshape(FRAMES, ROWS, HEADS, HEAD_DIM)
        padding = jnp.zeros((HALO, ROWS, HEADS, HEAD_DIM), jnp.bfloat16)
        keys_padded = jnp.concatenate([padding, keys_all, padding], axis=0)
        values_padded = jnp.concatenate([padding, values_all, padding], axis=0)

        def attend_frame(frame_index):
            query_rows = lax.dynamic_index_in_dim(queries, frame_index, 0, keepdims=False).astype(jnp.float32)
            key_rows = lax.dynamic_slice_in_dim(keys_padded, frame_index, 2 * HALO + 1, 0).reshape((2 * HALO + 1) * ROWS, HEADS, HEAD_DIM).astype(jnp.float32)
            value_rows = lax.dynamic_slice_in_dim(values_padded, frame_index, 2 * HALO + 1, 0).reshape((2 * HALO + 1) * ROWS, HEADS, HEAD_DIM).astype(jnp.float32)
            reach_width = lax.dynamic_index_in_dim(window_width, frame_index, 0, keepdims=False)
            key_frame = frame_index + offsets
            inside = (jnp.abs(offsets) <= reach_width) & (key_frame >= 0) & (key_frame < FRAMES)
            allowed = jnp.repeat(inside, ROWS, total_repeat_length=(2 * HALO + 1) * ROWS)
            scores = jnp.einsum('qhd,khd->hqk', query_rows, key_rows) / math.sqrt(HEAD_DIM)
            scores = jnp.where(allowed[None, None, :], scores, -1e+30)
            row_max = lax.optimization_barrier(jnp.max(scores, axis=-1, keepdims=True))
            weights_exp = jnp.exp(scores - row_max)
            weights = (weights_exp / lax.optimization_barrier(jnp.sum(weights_exp, axis=-1, keepdims=True))).astype(jnp.bfloat16)
            mixed = jnp.einsum('hqk,khd->qhd', weights.astype(jnp.float32), value_rows)
            return mixed.astype(jnp.bfloat16).reshape(ROWS, D)
        mixed_all = lax.map(attend_frame, jnp.arange(FRAMES, dtype=jnp.int32))
        projected = jnp.dot(mixed_all.reshape(FRAMES * ROWS, D), w_out, preferred_element_type=jnp.float32).reshape(FRAMES, ROWS, D)
        velocity = float_state + gate_rows * projected
        outputs.append(velocity.astype(jnp.bfloat16))
        updated = (float_state + (sigma_next - sigma_here)[:, None, None] * velocity).astype(jnp.bfloat16)
        latent = jnp.concatenate([updated[1:], fresh_noise[step_index][None]], axis=0)
    return (latent, jnp.stack(outputs))
```

```python
import functools
import math

import jax
import jax.numpy as jnp
from jax import lax
from jax.experimental import pallas as pl
from jax.experimental.pallas import tpu as pltpu
from jax.sharding import PartitionSpec as P

HEAD_DIM = 128
HALO = 2
STRIDE = 8
NORM_EPS = 1e-06
BF16 = jnp.bfloat16
F32 = jnp.float32
VMEM_LIMIT = 48 * 1024 * 1024


def sigma_of(level, levels):
    share = level.astype(F32) / levels
    return 5.0 * share / (1.0 + 4.0 * share)


def embed_levels(level, half_width):
    index_k = jnp.arange(half_width, dtype=F32)
    frequency = jnp.exp(-math.log(10000.0) * index_k / half_width)
    phase = level.astype(F32)[..., None] * frequency
    return jnp.concatenate([jnp.cos(phase), jnp.sin(phase)], axis=-1).astype(BF16)


def dot(a, b):
    return jnp.dot(a, b, preferred_element_type=F32)


def call(body, meta, args, specs, outs, scratch=(), flops=0):
    in_specs = []
    nbytes = 0
    for a, s in zip(args, specs):
        if s is None:
            s = pl.BlockSpec(a.shape, functools.partial(lambda n, *_: (0,) * n, a.ndim))
        in_specs.append(s)
        nbytes += math.prod(s.block_shape) * a.dtype.itemsize
    out_specs = [
        pl.BlockSpec(o.shape, functools.partial(lambda n, *_: (0,) * n, len(o.shape)))
        for o in outs
    ]
    nbytes += sum(math.prod(o.shape) * o.dtype.itemsize for o in outs)
    return pl.pallas_call(
        body,
        grid_spec=pltpu.PrefetchScalarGridSpec(
            num_scalar_prefetch=len(meta),
            grid=(1,),
            in_specs=in_specs,
            out_specs=out_specs,
            scratch_shapes=scratch,
        ),
        out_shape=outs,
        compiler_params=pltpu.CompilerParams(vmem_limit_bytes=VMEM_LIMIT),
        cost_estimate=pl.CostEstimate(flops=flops, bytes_accessed=nbytes, transcendentals=0),
    )(*meta, *args)


def normalize(mine, theirs, scale_mine, shift_mine, scale_theirs, shift_theirs, out_ref):
    a = mine.astype(F32)
    b = theirs.astype(F32)
    half = a.shape[1]
    width = 2 * half
    total = jnp.sum(a, axis=-1, keepdims=True) + jnp.sum(b, axis=-1, keepdims=True)
    square = jnp.sum(a * a, axis=-1, keepdims=True) + jnp.sum(b * b, axis=-1, keepdims=True)
    mean = total / width
    inv = lax.rsqrt(square / width - mean * mean + NORM_EPS)
    out_ref[:, :half] = ((a - mean) * inv * (1.0 + scale_mine) + shift_mine).astype(BF16)
    out_ref[:, half:] = ((b - mean) * inv * (1.0 + scale_theirs) + shift_theirs).astype(BF16)


def norm_body(slots, meta_ref, *refs):
    count = len(slots)
    mod_m, mod_t = refs[2 * count : 2 * count + 2]
    for i, slot in enumerate(slots):
        normalize(
            refs[2 * i][...],
            refs[2 * i + 1][...],
            mod_m[slot * 3 + 1 : slot * 3 + 2, :],
            mod_m[slot * 3 : slot * 3 + 1, :],
            mod_t[slot * 3 + 1 : slot * 3 + 2, :],
            mod_t[slot * 3 : slot * 3 + 1, :],
            refs[2 * count + 2 + i],
        )


def project(frame_ref, w_mine, w_theirs):
    half = w_mine.shape[0]
    return (
        dot(frame_ref[:, :half], w_mine[...]) + dot(frame_ref[:, half:], w_theirs[...])
    ).astype(BF16)


def local_body(meta_ref, own, other, wq_m, wq_t, wk_m, wk_t, wv_m, wv_t, q_ref, k_ref, v_ref):
    for i, frame in enumerate((own, other)):
        k_ref[i] = project(frame, wk_m, wk_t)
        v_ref[i] = project(frame, wv_m, wv_t)
        q_ref[i] = project(frame, wq_m, wq_t)


def attend_body(
    step, queue, meta_ref, width_ref,
    a_own, a_other, b_own, b_other, wk_m, wk_t, wv_m, wv_t, q_ref, kl_ref, vl_ref,
    own_out, other_out, ks, vs,
):
    place = meta_ref[2]
    behind = meta_ref[3]
    for i in range(2):
        ks[i] = kl_ref[i]
        vs[i] = vl_ref[i]
    for i, frame in enumerate((a_own, a_other, b_own, b_other)):
        ks[2 + i] = project(frame, wk_m, wk_t)
        vs[2 + i] = project(frame, wv_m, wv_t)
    factor = math.log2(math.e) / math.sqrt(HEAD_DIM)
    for qi, out in enumerate((own_out, other_out)):
        here = place ^ qi
        slot = (here - step) & (queue - 1)
        reach = width_ref[slot]
        index, allowed = [], []
        for offset in range(-HALO, HALO + 1):
            there = (here + offset) & (queue - 1)
            pick = jnp.int32(5)
            for j, known in enumerate((place, place ^ 1, place ^ 2, place ^ 3, behind)):
                pick = jnp.where(there == known, j, pick)
            index.append(pick)
            key_slot = slot + offset
            allowed.append((abs(offset) <= reach) & (key_slot >= 0) & (key_slot < queue))
        for head in range(ks.shape[2] // HEAD_DIM):
            lanes = slice(head * HEAD_DIM, (head + 1) * HEAD_DIM)
            query = q_ref[qi, :, lanes]
            scores = []
            for j in range(2 * HALO + 1):
                s = lax.dot_general(
                    query, ks[index[j], :, lanes], (((1,), (1,)), ((), ())),
                    preferred_element_type=F32,
                )
                scores.append(jnp.where(allowed[j], s, -1e30))
            top = functools.reduce(jnp.maximum, scores)
            top = jnp.max(top, axis=-1, keepdims=True) * factor
            total = None
            mixed = None
            for j in range(2 * HALO + 1):
                w = jnp.exp2(scores[j] * factor - top)
                total = w if total is None else total + w
                part = dot(w.astype(BF16), vs[index[j], :, lanes])
                mixed = part if mixed is None else mixed + part
            total = jnp.sum(total, axis=-1, keepdims=True)
            out[:, lanes] = (mixed / total).astype(BF16)


def out_step_body(
    meta_ref, change_ref,
    m_self, m_core, m_y, m_yx,
    w_s0, w_c0, w_y0, w_x0, w_s1, w_c1, w_y1, w_x1,
    lat_m, lat_t, fresh_m, fresh_t, mod_m, mod_t,
    vel_ref, upd_ref, normed_ref,
):
    change = change_ref[0]
    first = meta_ref[2] == 0
    nexts = []
    for half, (ws, wc, wy, wx, lat, fresh, mod) in enumerate((
        (w_s0, w_c0, w_y0, w_x0, lat_m, fresh_m, mod_m),
        (w_s1, w_c1, w_y1, w_x1, lat_t, fresh_t, mod_t),
    )):
        proj = dot(m_self[...], ws[...]) + dot(m_core[...], wc[...])
        proj += dot(m_y[...], wy[...]) + dot(m_yx[...], wx[...])
        state = lat[...].astype(F32)
        velocity = state + mod[2:3, :] * proj
        updated = (state + change * velocity).astype(BF16)
        if half == 0:
            vel_ref[...] = velocity.astype(BF16)
            upd_ref[...] = updated
        nexts.append(jnp.where(first, fresh[...].astype(F32), updated.astype(F32)))
    normalize(
        nexts[0], nexts[1],
        mod_m[10:11, :], mod_m[9:10, :], mod_t[10:11, :], mod_t[9:10, :],
        normed_ref,
    )


def out_last_body(
    meta_ref, change_ref,
    m_self, m_core, m_y, m_yx, w_s0, w_c0, w_y0, w_x0, shifted, fresh, mod_m,
    vel_ref, upd_ref,
):
    change = change_ref[0]
    last = meta_ref[4] == 1
    proj = dot(m_self[...], w_s0[...]) + dot(m_core[...], w_c0[...])
    proj += dot(m_y[...], w_y0[...]) + dot(m_yx[...], w_x0[...])
    state = jnp.where(last, fresh[0].astype(F32), shifted[...].astype(F32))
    velocity = state + mod_m[2:3, :] * proj
    vel_ref[...] = velocity.astype(BF16)
    upd_ref[...] = (state + change * velocity).astype(BF16)


def per_device(
    latents, fresh_noise, level_index, window_width, w_mod, w_query, w_key, w_value, w_out
):
    queue = lax.axis_size("queue")
    place = lax.axis_index("queue")
    side = lax.axis_index("heads")
    core = place & 1
    chip = place >> 1
    behind_of = lambda f: ((((f >> 1) + (1 if (f >> 1) & 1 else -1)) % (queue // 2)) << 1) | (f & 1)
    behind = (((jnp.where(chip & 1 == 1, chip + 1, chip - 1) & (queue // 2 - 1)) << 1) | core)
    meta = jnp.stack(
        [side, core, place, behind, (place == queue - 1).astype(jnp.int32)]
    ).astype(jnp.int32)

    rows, half = latents.shape[1:]
    group = half // 2
    freq = w_mod.shape[0]
    slots = range(queue)

    core_swap = [(f, f ^ 1) for f in slots]
    near = [(f, f ^ 2) for f in slots]
    far_open = [(f, behind_of(f)) for f in slots if abs(behind_of(f) - f) <= 2]
    far_ring = [(f, behind_of(f)) for f in slots]
    sides = [(0, 1), (1, 0)]
    both = ("queue", "heads")

    def on_queue(x, perm):
        return lax.ppermute(x, "queue", perm)

    def on_sides(x):
        return lax.ppermute(x, "heads", sides)

    mine = latents[0]
    theirs = on_sides(mine)
    near_mine = on_queue(mine, near)
    far_mine = on_queue(mine, far_open)

    w_send = lax.dynamic_slice_in_dim(w_out, core * group, group, 0)
    w_far_core = lax.ppermute(
        w_send, both, [(f * 2 + h, (f ^ (queue // 2)) * 2 + 1 - h) for f in slots for h in (0, 1)]
    )
    fresh_theirs = lax.ppermute(fresh_noise[0], both, [(0, 1), (1, 0)])

    levels = [
        lax.dynamic_index_in_dim(level_index, p, 0, keepdims=False)
        for p in (place, place ^ 2, behind, (place - 1) & (queue - 1))
    ]
    embedding = embed_levels(jnp.stack(levels), freq // 2)
    mod_mine = dot(embedding, w_mod.reshape(freq, 3 * half)).reshape(12, half)
    mod_theirs = on_sides(mod_mine)
    sigma_here = sigma_of(levels[0], queue * STRIDE)
    sigma_next = jnp.where(place > 0, sigma_of(levels[3], queue * STRIDE), 0.0)
    change = (sigma_next - sigma_here).reshape(1)

    frame = jax.ShapeDtypeStruct((rows, 2 * half), BF16)
    half_frame = jax.ShapeDtypeStruct((rows, half), BF16)
    piece = jax.ShapeDtypeStruct((rows, group), BF16)
    pair = jax.ShapeDtypeStruct((2, rows, group), BF16)

    def in_mine():
        return pl.BlockSpec((half, group), lambda i, m, *_: (m[0], m[1]))

    def in_theirs():
        return pl.BlockSpec((half, group), lambda i, m, *_: (1 - m[0], m[1]))

    def normed(pairs, which):
        args = [x for p in pairs for x in p] + [mod_mine, mod_theirs]
        return call(
            functools.partial(norm_body, which), [meta], args, [None] * len(args),
            [frame] * len(pairs),
        )

    def attention(step, own, near_own, far_own):
        other = on_queue(own, core_swap)
        q, k, v = call(
            local_body, [meta],
            [own, other, w_query, w_query, w_key, w_key, w_value, w_value],
            [None, None] + [in_mine(), in_theirs()] * 3,
            [pair] * 3, flops=2 * 2 * rows * 2 * half * 3 * group,
        )
        near_other = on_queue(near_own, core_swap)
        far_other = on_queue(far_own, core_swap)
        return call(
            functools.partial(attend_body, step, queue), [meta, window_width],
            [near_own, near_other, far_own, far_other, w_key, w_key, w_value, w_value, q, k, v],
            [None] * 4 + [in_mine(), in_theirs()] * 2 + [None] * 3,
            [piece, piece],
            scratch=[pltpu.VMEM((6, rows, group), BF16)] * 2,
            flops=2 * 4 * rows * 2 * half * 2 * group + 4 * 2 * rows * 5 * rows * group,
        )

    def w_specs(flip):
        col = (lambda m: 1 - m[0]) if flip else (lambda m: m[0])
        return [
            pl.BlockSpec((group, half), lambda i, m, *_: (m[1], col(m))),
            pl.BlockSpec((group, half), lambda i, m, *_: (1 - m[1], col(m))),
            pl.BlockSpec((group, half), lambda i, m, *_: (0, col(m))),
            pl.BlockSpec((group, half), lambda i, m, *_: (0, col(m))),
        ]

    near_theirs = on_sides(near_mine)
    far_theirs = on_queue(theirs, far_open)
    (own,) = normed([(mine, theirs)], [0])
    near_own, far_own = normed([(near_mine, near_theirs), (far_mine, far_theirs)], [1, 2])
    w_far_other = on_queue(w_far_core, core_swap)
    m_own, m_other = attention(0, own, near_own, far_own)
    m_core = on_queue(m_other, core_swap)
    m_y = on_sides(m_own)
    m_yx = lax.ppermute(
        m_other, both, [(f * 2 + h, (f ^ 1) * 2 + 1 - h) for f in slots for h in (0, 1)]
    )
    weights = [w_out, w_out, w_far_core, w_far_other]
    vel0, upd0, own = call(
        out_step_body, [meta, change],
        [m_own, m_core, m_y, m_yx] + weights * 2
        + [mine, theirs, fresh_noise[0], fresh_theirs, mod_mine, mod_theirs],
        [None] * 4 + w_specs(False) + w_specs(True) + [None] * 6,
        [half_frame, half_frame, frame], flops=2 * rows * 4 * half * half,
    )

    near_own = on_queue(own, near)
    far_own = on_queue(own, far_ring)
    m_own, m_other = attention(1, own, near_own, far_own)
    shifted = on_queue(upd0, [(f, f - 1) for f in slots if f > 0])

    def back(f):
        return f - 1 if f & 1 else (f - 1) % queue

    def keep(f):
        return (f - 2) % queue if f & 1 else f

    def crossed(to):
        return [(f * 2 + h, to(f) * 2 + 1 - h) for f in slots for h in (0, 1)]

    m_core = on_queue(m_own, [(f, back(f)) for f in slots])
    m_self = on_queue(m_other, [(f, keep(f)) for f in slots])
    m_yx = lax.ppermute(m_own, both, crossed(back))
    m_y = lax.ppermute(m_other, both, crossed(keep))
    vel1, upd1 = call(
        out_last_body, [meta, change],
        [m_self, m_core, m_y, m_yx] + weights + [shifted, fresh_noise, mod_mine],
        [None] * 4 + w_specs(False) + [None] * 3,
        [half_frame, half_frame], flops=2 * rows * 2 * half * half,
    )
    arrived = on_queue(upd1, [(f, f - 1) for f in slots if f > 0])
    latent = jnp.where(place == queue - 1, fresh_noise[1], arrived)
    return (latent[None], jnp.stack([vel0, vel1])[:, None])


def solution(mesh):
    in_specs = (
        P("queue", None, "heads"),
        P(None, None, "heads"),
        P(),
        P(),
        P(None, None, "heads"),
        P(None, "heads"),
        P(None, "heads"),
        P(None, "heads"),
        P("heads", None),
    )
    out_specs = (P("queue", None, "heads"), P(None, "queue", None, "heads"))
    return jax.shard_map(
        per_device, mesh=mesh, in_specs=in_specs, out_specs=out_specs, check_vma=False
    )
```

```python
import functools
import math

import jax
import jax.numpy as jnp
from jax import lax
from jax.experimental import pallas as pl
from jax.experimental.pallas import tpu as pltpu
from jax.sharding import PartitionSpec as P

HEAD_DIM = 128
STRIDE = 8
NORM_EPS = 1e-06
BF16 = jnp.bfloat16
F32 = jnp.float32
VMEM_LIMIT = 32 * 1024 * 1024
SCORE_FACTOR = math.log2(math.e) / math.sqrt(HEAD_DIM)
SHIFT, SCALE, GATE, CHANGE = 0, 4, 8, 12


def dot(a, b):
    return jnp.dot(a, b, preferred_element_type=F32)


def whole(shape):
    return pl.BlockSpec(shape, functools.partial(lambda n, *_: (0,) * n, len(shape)))


def call(body, meta, args, specs, outs, scratch=(), flops=0):
    in_specs = [whole(a.shape) if s is None else s for a, s in zip(args, specs)]
    nbytes = sum(math.prod(s.block_shape) * a.dtype.itemsize for a, s in zip(args, in_specs))
    nbytes += sum(math.prod(o.shape) * o.dtype.itemsize for o in outs)
    return pl.pallas_call(
        body,
        grid_spec=pltpu.PrefetchScalarGridSpec(
            num_scalar_prefetch=len(meta),
            grid=(1,),
            in_specs=in_specs,
            out_specs=[whole(o.shape) for o in outs],
            scratch_shapes=scratch,
        ),
        out_shape=outs,
        compiler_params=pltpu.CompilerParams(vmem_limit_bytes=VMEM_LIMIT),
        cost_estimate=pl.CostEstimate(flops=1, bytes_accessed=1, transcendentals=0),
    )(*meta, *args)


def sigma_of(level, levels):
    share = level / levels
    return 5.0 * share / (1.0 + 4.0 * share)


def prepare_body(queue, meta_ref, level_ref, w_mod, mod_ref):
    place, behind = meta_ref[2], meta_ref[3]
    before = (place - 1) & (queue - 1)
    here = level_ref[place]
    rows = lax.broadcasted_iota(jnp.int32, (16, w_mod.shape[1] // 2), 0)
    level = jnp.zeros(rows.shape, jnp.int32)
    for i, value in enumerate((here, level_ref[place ^ 2], level_ref[behind], level_ref[before])):
        level = jnp.where(rows == i, value, level)
    freqs = w_mod.shape[1] // 2
    index_k = lax.broadcasted_iota(jnp.int32, (16, freqs), 1).astype(F32)
    phase = level.astype(F32) * jnp.exp(-math.log(10000.0) * index_k / freqs)
    low = jnp.cos(phase).astype(BF16)
    high = jnp.sin(phase).astype(BF16)
    for kind in range(3):
        table = dot(low, w_mod[kind, :freqs, :]) + dot(high, w_mod[kind, freqs:, :])
        mod_ref[4 * kind : 4 * kind + 4, :] = table[:4, :]
    shape = (4, mod_ref.shape[1])
    levels = queue * STRIDE
    sigma_here = sigma_of(jnp.full(shape, here, jnp.int32).astype(F32), levels)
    sigma_next = sigma_of(jnp.full(shape, level_ref[before], jnp.int32).astype(F32), levels)
    mod_ref[CHANGE : CHANGE + 4, :] = jnp.where(place > 0, sigma_next, 0.0) - sigma_here


def copy_body(meta_ref, w_rows, fresh, wide_ref, narrow_ref, fresh_ref):
    fresh_ref[...] = fresh[0]
    wide = wide_ref.shape[0]
    wide_ref[...] = w_rows[:wide, :]
    narrow_ref[...] = w_rows[wide:, :]


def lane_block(index, width):
    return pl.ds(pl.multiple_of(index * width, HEAD_DIM), width)


def normalize(a, b, mod_a, mod_b, slot, side, *out_refs):
    a = a.astype(F32)
    b = b.astype(F32)
    half = a.shape[1]
    width = 2 * half
    total = jnp.sum(a, axis=-1, keepdims=True) + jnp.sum(b, axis=-1, keepdims=True)
    square = jnp.sum(a * a, axis=-1, keepdims=True) + jnp.sum(b * b, axis=-1, keepdims=True)
    mean = total / width
    inv = lax.rsqrt(square / width - mean * mean + NORM_EPS)
    for x, mod, at in ((a, mod_a, side), (b, mod_b, 1 - side)):
        scale, shift = mod(SCALE + slot), mod(SHIFT + slot)
        x = ((x - mean) * inv * (1.0 + scale) + shift).astype(BF16)
        for i, out_ref in enumerate(out_refs):
            count = out_ref.shape[0]
            out_ref[:, lane_block(at, half)] = x[i * count : (i + 1) * count, :]


def norm_body(jobs, meta_ref, *refs):
    count = len(jobs)
    mod_m, mod_t = refs[2 * count : 2 * count + 2]
    for i, (slot, may_cross) in enumerate(jobs):
        side = meta_ref[0]
        row_m = lambda r: mod_m[r : r + 1, :]
        row_t = lambda r: mod_t[r : r + 1, :]
        if may_cross:
            crossed = meta_ref[5] == 1
            side = side ^ meta_ref[5]
            mod_a = lambda r: jnp.where(crossed, row_t(r), row_m(r))
            mod_b = lambda r: jnp.where(crossed, row_m(r), row_t(r))
        else:
            mod_a, mod_b = row_m, row_t
        normalize(
            refs[2 * i][...], refs[2 * i + 1][...], mod_a, mod_b, slot, side,
            refs[2 * count + 2 + i],
        )


def lane_max(scores, allowed):
    best = None
    for s, ok in zip(scores, allowed):
        top = s[:, :HEAD_DIM]
        for at in range(HEAD_DIM, s.shape[1], HEAD_DIM):
            top = jnp.maximum(top, s[:, at : at + HEAD_DIM])
        top = jnp.where(ok, top, -1e30)
        best = top if best is None else jnp.maximum(best, top)
    return jnp.max(best, axis=-1, keepdims=True)


def weigh(scores, allowed, top, values):
    total, mixed = None, None
    for s, ok, v in zip(scores, allowed, values):
        w = jnp.exp2(s - jnp.where(ok, top, 1e30))
        part = w[:, :HEAD_DIM]
        for at in range(HEAD_DIM, s.shape[1], HEAD_DIM):
            part = part + w[:, at : at + HEAD_DIM]
        total = part if total is None else total + part
        product = dot(w.astype(BF16), v)
        mixed = product if mixed is None else mixed + product
    return jnp.sum(total, axis=-1, keepdims=True), mixed


def scores_of(query, keys):
    return lax.dot_general(query, keys, (((1,), (1,)), ((), ())), preferred_element_type=F32)


def within(slot, offset, reach, queue):
    at = slot + offset
    return (jnp.abs(offset) <= reach) & (at >= 0) & (at < queue)


def local_body(
    step, queue, parts, meta_ref, width_ref, *refs
):
    frames = refs[:parts], refs[parts : 2 * parts]
    wq, wk, wv, q_ref, acc_ref, stat_ref, ks, vs = refs[2 * parts :]
    place = meta_ref[2]
    for i, pieces in enumerate(frames):
        for j, piece in enumerate(pieces):
            count = piece.shape[0]
            at = slice(j * count, (j + 1) * count)
            ks[i, at, :] = dot(piece[...], wk[...]).astype(BF16)
            vs[i, at, :] = dot(piece[...], wv[...]).astype(BF16)
            q_ref[i, at, :] = (dot(piece[...], wq[...]) * SCORE_FACTOR).astype(BF16)
    for qi in range(2):
        here = place ^ qi
        slot = (here - step) & (queue - 1)
        reach = width_ref[slot]
        aside = 1 - 2 * (here & 1)
        allowed = (reach >= 0, within(slot, aside, reach, queue))
        for head in range(ks.shape[2] // HEAD_DIM):
            lanes = slice(head * HEAD_DIM, (head + 1) * HEAD_DIM)
            query = q_ref[qi, :, lanes]
            scores = [scores_of(query, ks[j, :, lanes]) for j in (qi, 1 - qi)]
            top = lane_max(scores, allowed)
            total, mixed = weigh(scores, allowed, top, [vs[j, :, lanes] for j in (qi, 1 - qi)])
            acc_ref[qi, :, lanes] = mixed
            stat_ref[qi, :, head : head + 1] = top
            stat_ref[qi, :, 8 + head : 9 + head] = total


def halo_body(
    step, queue, final, meta_ref, width_ref,
    a_own, a_other, b_own, b_other, wk, wv, q_ref, acc_in, stat_in, *rest,
):
    outs, (ks, vs) = rest[:-2], rest[-2:]
    place, behind = meta_ref[2], meta_ref[3]
    for i, frame in enumerate((a_own, a_other, b_own, b_other)):
        ks[i] = dot(frame[...], wk[...]).astype(BF16)
        vs[i] = dot(frame[...], wv[...]).astype(BF16)
    for qi in range(2):
        here = place ^ qi
        slot = (here - step) & (queue - 1)
        reach = width_ref[slot]
        index, allowed = [], []
        for offset in (-2, 2, 2 * (here & 1) - 1):
            there = (here + offset) & (queue - 1)
            pick = jnp.int32(3)
            for j, known in enumerate((place ^ 2, place ^ 3, behind)):
                pick = jnp.where(there == known, j, pick)
            index.append(pick)
            allowed.append(within(slot, jnp.int32(offset), reach, queue))
        for head in range(ks.shape[2] // HEAD_DIM):
            lanes = slice(head * HEAD_DIM, (head + 1) * HEAD_DIM)
            query = q_ref[qi, :, lanes]
            scores = [scores_of(query, ks[j, :, lanes]) for j in index]
            before = stat_in[qi, :, head : head + 1]
            top = jnp.maximum(before, lane_max(scores, allowed))
            total, mixed = weigh(scores, allowed, top, [vs[j, :, lanes] for j in index])
            fade = jnp.exp2(before - top)
            total = total + fade * stat_in[qi, :, 8 + head : 9 + head]
            mixed = mixed + fade * acc_in[qi, :, lanes]
            if final:
                outs[qi][:, lanes] = (mixed / total).astype(BF16)
            else:
                outs[0][qi, :, lanes] = mixed
                outs[1][qi, :, head : head + 1] = top
                outs[1][qi, :, 8 + head : 9 + head] = total


def output_sums(mixed, weights):
    m_self, m_core, m_y, m_yx = mixed
    w_self, w_core, w_y0, w_y1, w_x0, w_x1 = weights
    wide = w_y0.shape[0]
    sums = dot(m_self[...], w_self[...]) + dot(m_core[...], w_core[...])
    sums += dot(m_y[:, :wide], w_y0[...]) + dot(m_y[:, wide:], w_y1[...])
    return sums + dot(m_yx[:, :wide], w_x0[...]) + dot(m_yx[:, wide:], w_x1[...])


def out_step_body(
    meta_ref,
    m_self, m_core, m_y, m_yx, *rest,
):
    lat_m, lat_t, fresh_m, fresh_t, mod_m, mod_t, vel_ref, upd_ref, *normed_refs = rest[12:]
    mixed = m_self, m_core, m_y, m_yx
    change = mod_m[CHANGE : CHANGE + 1, :]
    first = meta_ref[2] == 0
    fresh = (fresh_m[0], fresh_t[...])
    nexts = []
    for side, (lat, mod) in enumerate(((lat_m, mod_m), (lat_t, mod_t))):
        proj = output_sums(mixed, rest[6 * side : 6 * side + 6])
        state = lat[...].astype(F32)
        velocity = state + mod[GATE : GATE + 1, :] * proj
        updated = (state + change * velocity).astype(BF16)
        if side == 0:
            vel_ref[...] = velocity.astype(BF16)
            upd_ref[...] = updated
        nexts.append(jnp.where(first, fresh[side].astype(F32), updated.astype(F32)))
    normalize(
        nexts[0], nexts[1], lambda r: mod_m[r : r + 1, :], lambda r: mod_t[r : r + 1, :],
        3, meta_ref[0], *normed_refs,
    )


def out_last_body(
    meta_ref,
    m_self, m_core, m_y, m_yx, *rest,
):
    shifted, fresh, mod_m, vel_first, vel_ref, upd_ref = rest[6:]
    last = meta_ref[4] == 1
    proj = output_sums((m_self, m_core, m_y, m_yx), rest[:6])
    state = jnp.where(last, fresh[0].astype(F32), shifted[...].astype(F32))
    velocity = state + mod_m[GATE : GATE + 1, :] * proj
    vel_ref[0] = vel_first[...]
    vel_ref[1] = velocity.astype(BF16)
    upd_ref[...] = (state + mod_m[CHANGE : CHANGE + 1, :] * velocity).astype(BF16)


def tie(*arrays):
    return lax.optimization_barrier(arrays)


def per_device(
    latents, fresh_noise, level_index, window_width, w_mod, w_query, w_key, w_value, w_out
):
    queue = lax.axis_size("queue")
    place = lax.axis_index("queue")
    side = lax.axis_index("heads")
    core = place & 1
    chips = queue // 2

    def behind_of(f):
        chip = f >> 1
        return (((chip + 1 if chip & 1 else chip - 1) % chips) << 1) | (f & 1)

    chip = place >> 1
    behind = ((jnp.where(chip & 1 == 1, chip + 1, chip - 1) & (chips - 1)) << 1) | core
    crossed = ((place ^ behind) // chips) & 1
    meta = jnp.stack(
        [side, core, place, behind, (place == queue - 1).astype(jnp.int32), crossed]
    ).astype(jnp.int32)

    rows, half = latents.shape[1:]
    group = half // 2
    wide = group - HEAD_DIM
    slots = range(queue)

    core_swap = [(f, f ^ 1) for f in slots]
    near = [(f, f ^ 2) for f in slots]
    far_ring = [
        (f * 2 + h, behind_of(f) * 2 + (h ^ (((f ^ behind_of(f)) // chips) & 1)))
        for f in slots
        for h in (0, 1)
    ]
    far_open = [(s, d if abs(s // 2 - d // 2) <= 2 else s ^ 1) for s, d in far_ring]
    step_down = [(f * 2 + h, f * 2 + h - 2 if f else queue * 2 - 1 - h) for f in slots for h in (0, 1)]
    both = ("queue", "heads")

    def on_queue(x, perm):
        return lax.ppermute(x, "queue", perm)

    def on_sides(x):
        return lax.ppermute(x, "heads", [(0, 1), (1, 0)])

    def on_both(x, perm):
        return lax.ppermute(x, both, perm)

    def aside(to):
        return [(f * 2 + h, to(f) * 2 + 1 - h) for f in slots for h in (0, 1)]

    frame = jax.ShapeDtypeStruct((rows, 2 * half), BF16)
    half_frame = jax.ShapeDtypeStruct((rows, half), BF16)
    piece = jax.ShapeDtypeStruct((rows, group), BF16)
    pair = jax.ShapeDtypeStruct((2, rows, group), BF16)
    sums = jax.ShapeDtypeStruct((2, rows, group), F32)
    stats = jax.ShapeDtypeStruct((2, rows, HEAD_DIM), F32)

    def columns():
        return pl.BlockSpec((2 * half, group), lambda i, m, *_: (0, m[1]))

    def fresh_spec(step):
        return pl.BlockSpec((1, rows, half), lambda *_: (step, 0, 0))

    mine = latents[0]
    theirs = on_sides(mine)
    near_mine = on_queue(mine, near)
    far_mine = on_both(mine, far_open)

    (mod_mine,) = call(
        functools.partial(prepare_body, queue), [meta, level_index],
        [jnp.transpose(w_mod, (1, 0, 2))], [None],
        [jax.ShapeDtypeStruct((16, half), F32)],
    )
    mod_theirs = on_sides(mod_mine)
    near_mine, far_mine, theirs, mod_mine = tie(near_mine, far_mine, theirs, mod_mine)

    def normed(pairs, jobs):
        args = [x for p in pairs for x in p] + [mod_mine, mod_theirs]
        return call(
            functools.partial(norm_body, jobs), [meta], args, [None] * len(args),
            [frame] * len(pairs),
        )

    def local(step, own):
        other = [on_queue(x, core_swap) for x in own]
        return call(
            functools.partial(local_body, step, queue, len(own)), [meta, window_width],
            own + other + [w_query, w_key, w_value], [None] * 2 * len(own) + [columns()] * 3,
            [pair, sums, stats],
            scratch=[pltpu.VMEM((2, rows, group), BF16)] * 2,
            flops=2 * 2 * rows * 2 * half * 3 * group + 4 * 2 * rows * 2 * rows * group,
        )

    def halo(step, near_own, far_own, state, final):
        count = near_own.shape[0]
        near_own, far_own, *state = tie(near_own, far_own, *state)
        near_other = on_queue(near_own, core_swap)
        far_other = on_queue(far_own, core_swap)
        return call(
            functools.partial(halo_body, step, queue, final), [meta, window_width],
            [near_own, near_other, far_own, far_other, w_key, w_value] + state,
            [None] * 4 + [columns()] * 2 + [None] * 3,
            [piece, piece] if final else [sums, stats],
            scratch=[pltpu.VMEM((4, count, group), BF16)] * 2,
            flops=2 * 4 * count * 2 * half * 2 * group + 4 * 2 * rows * 3 * count * group,
        )

    def w_specs(flip):
        col = (lambda m: 1 - m[0]) if flip else (lambda m: m[0])
        return [
            pl.BlockSpec((group, half), lambda i, m, *_: (m[1], col(m))),
            pl.BlockSpec((group, half), lambda i, m, *_: (1 - m[1], col(m))),
        ] + [
            pl.BlockSpec((n, half), lambda i, m, *_: (0, col(m))) for n in (wide, group - wide)
        ] * 2

    near_theirs = on_sides(near_mine)
    far_theirs = on_both(theirs, far_open)
    (own,) = normed([(mine, theirs)], [(0, False)])
    state = local(0, [own])
    near_theirs, far_theirs, *state = tie(near_theirs, far_theirs, *state)
    near_own, far_own = normed(
        [(near_mine, near_theirs), (far_mine, far_theirs)], [(1, False), (2, True)]
    )
    near_own, far_own, w_out_late = tie(near_own, far_own, w_out)
    send = call(
        copy_body, [meta], [w_out_late, fresh_noise],
        [pl.BlockSpec((group, 2 * half), lambda i, m, *_: (m[1], 0)), fresh_spec(0)],
        [jax.ShapeDtypeStruct((n, 2 * half), BF16) for n in (wide, group - wide)] + [half_frame],
    )
    far_weights = [on_both(send[0], aside(lambda f: f ^ chips)), on_sides(send[1])]
    fresh_theirs = on_sides(send[2])
    m_own, m_other = halo(0, near_own, far_own, state, True)
    m_y = on_sides(m_own)
    m_yx = on_both(m_other, aside(lambda f: f ^ 1))
    m_core = on_queue(m_other, core_swap)
    *far_weights, fresh_theirs, m_y = tie(*far_weights, fresh_theirs, m_y)
    far_weights_other = [on_queue(w, core_swap) for w in far_weights]
    weights = [w_out, w_out, *far_weights, *far_weights_other]
    vel0, upd0, *own = call(
        out_step_body, [meta],
        [m_own, m_core, m_y, m_yx] + weights * 2
        + [mine, theirs, fresh_noise, fresh_theirs, mod_mine, mod_theirs],
        [None] * 4 + w_specs(False) + w_specs(True) + [None, None, fresh_spec(0), None, None, None],
        [half_frame, half_frame, frame], flops=2 * rows * 4 * half * half,
    )

    (own,) = own
    near_own, far_own = on_queue(own, near), on_both(own, far_ring)
    state = local(1, [own])
    m_own, m_other = halo(1, near_own, far_own, state, True)
    upd0, _ = tie(upd0, m_own)
    shifted = on_both(upd0, step_down)

    def back(f):
        return (f - 1) % queue

    def keep(f):
        return (f - 2) % queue if f & 1 else f

    m_yx = on_both(m_own, aside(back))
    m_y = on_both(m_other, aside(keep))
    m_core = on_queue(m_own, [(f, back(f)) for f in slots])
    m_self = on_queue(m_other, [(f, keep(f)) for f in slots])
    vel, upd1 = call(
        out_last_body, [meta],
        [m_self, m_core, m_y, m_yx] + weights + [shifted, fresh_noise, mod_mine, vel0],
        [None] * 4 + w_specs(False) + [None, fresh_spec(0), None, None],
        [jax.ShapeDtypeStruct((2, rows, half), BF16), half_frame],
        flops=2 * rows * 2 * half * half,
    )
    arrived = on_both(upd1, step_down)
    latent = jnp.where(place == queue - 1, fresh_noise[1], arrived)
    return (latent[None], vel[:, None])


def solution(mesh):
    in_specs = (
        P("queue", None, "heads"),
        P(None, None, "heads"),
        P(),
        P(),
        P(None, None, "heads"),
        P(None, "heads"),
        P(None, "heads"),
        P(None, "heads"),
        P("heads", None),
    )
    out_specs = (P("queue", None, "heads"), P(None, "queue", None, "heads"))
    return jax.shard_map(
        per_device, mesh=mesh, in_specs=in_specs, out_specs=out_specs, check_vma=False
    )
```

```python
import functools
import math

import jax
import jax.numpy as jnp
from jax import lax
from jax.experimental import pallas as pl
from jax.experimental.pallas import tpu as pltpu
from jax.sharding import PartitionSpec as P

HEAD_DIM = 128
STRIDE = 8
NORM_EPS = 1e-06
BF16 = jnp.bfloat16
F32 = jnp.float32
VMEM_LIMIT = 32 * 1024 * 1024
SCORE_FACTOR = math.log2(math.e) / math.sqrt(HEAD_DIM)
SHIFT, SCALE, GATE, CHANGE = 0, 4, 8, 12


def dot(a, b):
    return jnp.dot(a, b, preferred_element_type=F32)


def whole(shape):
    return pl.BlockSpec(shape, functools.partial(lambda n, *_: (0,) * n, len(shape)))


def call(body, meta, args, specs, outs, scratch=(), flops=0):
    in_specs = [whole(a.shape) if s is None else s for a, s in zip(args, specs)]
    nbytes = sum(math.prod(s.block_shape) * a.dtype.itemsize for a, s in zip(args, in_specs))
    nbytes += sum(math.prod(o.shape) * o.dtype.itemsize for o in outs)
    return pl.pallas_call(
        body,
        grid_spec=pltpu.PrefetchScalarGridSpec(
            num_scalar_prefetch=len(meta),
            grid=(1,),
            in_specs=in_specs,
            out_specs=[whole(o.shape) for o in outs],
            scratch_shapes=scratch,
        ),
        out_shape=outs,
        compiler_params=pltpu.CompilerParams(vmem_limit_bytes=VMEM_LIMIT),
        cost_estimate=pl.CostEstimate(flops=1, bytes_accessed=1, transcendentals=0),
    )(*meta, *args)


def sigma_of(level, levels):
    share = level / levels
    return 5.0 * share / (1.0 + 4.0 * share)


def prepare_body(queue, meta_ref, level_ref, w_mod, mod_ref):
    place, behind = meta_ref[2], meta_ref[3]
    before = (place - 1) & (queue - 1)
    here = level_ref[place]
    rows = lax.broadcasted_iota(jnp.int32, (16, w_mod.shape[1] // 2), 0)
    level = jnp.zeros(rows.shape, jnp.int32)
    for i, value in enumerate((here, level_ref[place ^ 2], level_ref[behind], level_ref[before])):
        level = jnp.where(rows == i, value, level)
    freqs = w_mod.shape[1] // 2
    index_k = lax.broadcasted_iota(jnp.int32, (16, freqs), 1).astype(F32)
    phase = level.astype(F32) * jnp.exp(-math.log(10000.0) * index_k / freqs)
    low = jnp.cos(phase).astype(BF16)
    high = jnp.sin(phase).astype(BF16)
    for kind in range(3):
        table = dot(low, w_mod[kind, :freqs, :]) + dot(high, w_mod[kind, freqs:, :])
        mod_ref[4 * kind : 4 * kind + 4, :] = table[:4, :]
    levels = queue * STRIDE
    for i, slot in enumerate((place, before)):
        sigma = [
            sigma_of(jnp.full((1, mod_ref.shape[1]), level_ref[at], jnp.int32).astype(F32), levels)
            for at in (slot, (slot - 1) & (queue - 1))
        ]
        mod_ref[CHANGE + i : CHANGE + i + 1, :] = jnp.where(slot > 0, sigma[1], 0.0) - sigma[0]
    mod_ref[CHANGE + 2 :, :] = jnp.zeros((2, mod_ref.shape[1]), F32)


def copy_body(meta_ref, w_rows, wide_ref, narrow_ref):
    wide = wide_ref.shape[0]
    wide_ref[...] = w_rows[:wide, :]
    narrow_ref[...] = w_rows[wide:, :]


def lane_block(index, width):
    return pl.ds(pl.multiple_of(index * width, HEAD_DIM), width)


def normalize(a, b, mod_a, mod_b, slot, side, *out_refs):
    a = a.astype(F32)
    b = b.astype(F32)
    half = a.shape[1]
    width = 2 * half
    total = jnp.sum(a, axis=-1, keepdims=True) + jnp.sum(b, axis=-1, keepdims=True)
    square = jnp.sum(a * a, axis=-1, keepdims=True) + jnp.sum(b * b, axis=-1, keepdims=True)
    mean = total / width
    inv = lax.rsqrt(square / width - mean * mean + NORM_EPS)
    for x, mod, at in ((a, mod_a, side), (b, mod_b, 1 - side)):
        scale, shift = mod(SCALE + slot), mod(SHIFT + slot)
        x = ((x - mean) * inv * (1.0 + scale) + shift).astype(BF16)
        for i, out_ref in enumerate(out_refs):
            count = out_ref.shape[0]
            out_ref[:, lane_block(at, half)] = x[i * count : (i + 1) * count, :]


def norm_body(jobs, meta_ref, *refs):
    count = len(jobs)
    mod_m, mod_t = refs[2 * count : 2 * count + 2]
    for i, (slot, may_cross) in enumerate(jobs):
        side = meta_ref[0]
        row_m = lambda r: mod_m[r : r + 1, :]
        row_t = lambda r: mod_t[r : r + 1, :]
        if may_cross:
            crossed = meta_ref[4] == 1
            side = side ^ meta_ref[4]
            mod_a = lambda r: jnp.where(crossed, row_t(r), row_m(r))
            mod_b = lambda r: jnp.where(crossed, row_m(r), row_t(r))
        else:
            mod_a, mod_b = row_m, row_t
        normalize(
            refs[2 * i][...], refs[2 * i + 1][...], mod_a, mod_b, slot, side,
            refs[2 * count + 2 + i],
        )


def lane_max(scores, allowed):
    best = None
    for s, ok in zip(scores, allowed):
        top = s[:, :HEAD_DIM]
        for at in range(HEAD_DIM, s.shape[1], HEAD_DIM):
            top = jnp.maximum(top, s[:, at : at + HEAD_DIM])
        top = jnp.where(ok, top, -1e30)
        best = top if best is None else jnp.maximum(best, top)
    return jnp.max(best, axis=-1, keepdims=True)


def weigh(scores, allowed, top, values):
    total, mixed = None, None
    for s, ok, v in zip(scores, allowed, values):
        w = jnp.exp2(s - jnp.where(ok, top, 1e30))
        part = w[:, :HEAD_DIM]
        for at in range(HEAD_DIM, s.shape[1], HEAD_DIM):
            part = part + w[:, at : at + HEAD_DIM]
        total = part if total is None else total + part
        product = dot(w.astype(BF16), v)
        mixed = product if mixed is None else mixed + product
    return jnp.sum(total, axis=-1, keepdims=True), mixed


def scores_of(query, keys):
    return lax.dot_general(query, keys, (((1,), (1,)), ((), ())), preferred_element_type=F32)


def within(slot, offset, reach, queue):
    at = slot + offset
    return (jnp.abs(offset) <= reach) & (at >= 0) & (at < queue)


def local_body(
    step, queue, parts, meta_ref, width_ref, *refs
):
    frames = refs[:parts], refs[parts : 2 * parts]
    wq, wk, wv, q_ref, acc_ref, stat_ref, ks, vs = refs[2 * parts :]
    place = meta_ref[2]
    for i, pieces in enumerate(frames):
        for j, piece in enumerate(pieces):
            count = piece.shape[0]
            at = slice(j * count, (j + 1) * count)
            ks[i, at, :] = dot(piece[...], wk[...]).astype(BF16)
            vs[i, at, :] = dot(piece[...], wv[...]).astype(BF16)
            q_ref[i, at, :] = (dot(piece[...], wq[...]) * SCORE_FACTOR).astype(BF16)
    for qi in range(2):
        here = place ^ qi
        slot = (here - step) & (queue - 1)
        reach = width_ref[slot]
        aside = 1 - 2 * (here & 1)
        allowed = (reach >= 0, within(slot, aside, reach, queue))
        for head in range(ks.shape[2] // HEAD_DIM):
            lanes = slice(head * HEAD_DIM, (head + 1) * HEAD_DIM)
            query = q_ref[qi, :, lanes]
            scores = [scores_of(query, ks[j, :, lanes]) for j in (qi, 1 - qi)]
            top = lane_max(scores, allowed)
            total, mixed = weigh(scores, allowed, top, [vs[j, :, lanes] for j in (qi, 1 - qi)])
            acc_ref[qi, :, lanes] = mixed
            stat_ref[qi, :, head : head + 1] = top
            stat_ref[qi, :, 8 + head : 9 + head] = total


def halo_body(
    step, queue, final, meta_ref, width_ref,
    a_own, a_other, b_own, b_other, wk, wv, q_ref, acc_in, stat_in, *rest,
):
    outs, (ks, vs) = rest[:-2], rest[-2:]
    place, behind = meta_ref[2], meta_ref[3]
    for i, frame in enumerate((a_own, a_other, b_own, b_other)):
        ks[i] = dot(frame[...], wk[...]).astype(BF16)
        vs[i] = dot(frame[...], wv[...]).astype(BF16)
    for qi in range(2):
        here = place ^ qi
        slot = (here - step) & (queue - 1)
        reach = width_ref[slot]
        index, allowed = [], []
        for offset in (-2, 2, 2 * (here & 1) - 1):
            there = (here + offset) & (queue - 1)
            pick = jnp.int32(3)
            for j, known in enumerate((place ^ 2, place ^ 3, behind)):
                pick = jnp.where(there == known, j, pick)
            index.append(pick)
            allowed.append(within(slot, jnp.int32(offset), reach, queue))
        for head in range(ks.shape[2] // HEAD_DIM):
            lanes = slice(head * HEAD_DIM, (head + 1) * HEAD_DIM)
            query = q_ref[qi, :, lanes]
            scores = [scores_of(query, ks[j, :, lanes]) for j in index]
            before = stat_in[qi, :, head : head + 1]
            top = jnp.maximum(before, lane_max(scores, allowed))
            total, mixed = weigh(scores, allowed, top, [vs[j, :, lanes] for j in index])
            fade = jnp.exp2(before - top)
            total = total + fade * stat_in[qi, :, 8 + head : 9 + head]
            mixed = mixed + fade * acc_in[qi, :, lanes]
            if final:
                outs[qi][:, lanes] = (mixed / total).astype(BF16)
            else:
                outs[0][qi, :, lanes] = mixed
                outs[1][qi, :, head : head + 1] = top
                outs[1][qi, :, 8 + head : 9 + head] = total


def output_sums(mixed, weights):
    m_self, m_core, m_y, m_yx = mixed
    w_self, w_core, w_y0, w_y1, w_x0, w_x1 = weights
    wide = w_y0.shape[0]
    sums = dot(m_self[...], w_self[...]) + dot(m_core[...], w_core[...])
    sums += dot(m_y[:, :wide], w_y0[...]) + dot(m_y[:, wide:], w_y1[...])
    return sums + dot(m_yx[:, :wide], w_x0[...]) + dot(m_yx[:, wide:], w_x1[...])


def out_step_body(
    meta_ref,
    m_self, m_core, m_y, m_yx, *rest,
):
    lat_m, lat_t, fresh_m, fresh_t, mod_m, mod_t, vel_ref, next_ref, *normed_refs = rest[12:]
    mixed = m_self, m_core, m_y, m_yx
    change = mod_m[CHANGE : CHANGE + 1, :]
    first = meta_ref[2] == 0
    fresh = (fresh_m[0], fresh_t[...])
    nexts = []
    for side, (lat, mod) in enumerate(((lat_m, mod_m), (lat_t, mod_t))):
        proj = output_sums(mixed, rest[6 * side : 6 * side + 6])
        state = lat[...].astype(F32)
        velocity = state + mod[GATE : GATE + 1, :] * proj
        updated = (state + change * velocity).astype(BF16)
        if side == 0:
            vel_ref[...] = velocity.astype(BF16)
        nexts.append(jnp.where(first, fresh[side].astype(F32), updated.astype(F32)))
    next_ref[...] = nexts[0].astype(BF16)
    normalize(
        nexts[0], nexts[1], lambda r: mod_m[r : r + 1, :], lambda r: mod_t[r : r + 1, :],
        3, meta_ref[0], *normed_refs,
    )


def out_last_body(
    meta_ref,
    m_self, m_core, m_y, m_yx, *rest,
):
    latent, fresh, mod_m, vel_ref, upd_ref = rest[6:]
    proj = output_sums((m_self, m_core, m_y, m_yx), rest[:6])
    state = latent[...].astype(F32)
    velocity = state + mod_m[GATE + 3 : GATE + 4, :] * proj
    vel_ref[...] = velocity.astype(BF16)
    updated = state + mod_m[CHANGE + 1 : CHANGE + 2, :] * velocity
    leaves = meta_ref[2] == 1
    upd_ref[...] = jnp.where(leaves, fresh[0].astype(F32), updated).astype(BF16)


def tie(*arrays):
    return lax.optimization_barrier(arrays)


def per_device(
    latents, fresh_noise, level_index, window_width, w_mod, w_query, w_key, w_value, w_out
):
    queue = lax.axis_size("queue")
    place = lax.axis_index("queue")
    side = lax.axis_index("heads")
    core = place & 1
    chips = queue // 2

    def behind_of(f):
        chip = f >> 1
        return (((chip + 1 if chip & 1 else chip - 1) % chips) << 1) | (f & 1)

    chip = place >> 1
    behind = ((jnp.where(chip & 1 == 1, chip + 1, chip - 1) & (chips - 1)) << 1) | core
    crossed = ((place ^ behind) // chips) & 1
    meta = jnp.stack(
        [side, core, place, behind, crossed]
    ).astype(jnp.int32)

    rows, half = latents.shape[1:]
    group = half // 2
    wide = group - HEAD_DIM
    slots = range(queue)

    core_swap = [(f, f ^ 1) for f in slots]
    near = [(f, f ^ 2) for f in slots]
    far_ring = [
        (f * 2 + h, behind_of(f) * 2 + (h ^ (((f ^ behind_of(f)) // chips) & 1)))
        for f in slots
        for h in (0, 1)
    ]
    far_open = [(s, d if abs(s // 2 - d // 2) <= 2 else s) for s, d in far_ring]
    head_only = [(s, s ^ 1 if s < 2 else s) for s in range(2 * queue)]
    both = ("queue", "heads")

    def on_queue(x, perm):
        return lax.ppermute(x, "queue", perm)

    def on_sides(x):
        return lax.ppermute(x, "heads", [(0, 1), (1, 0)])

    def on_both(x, perm):
        return lax.ppermute(x, both, perm)

    def aside(to):
        return [(f * 2 + h, to(f) * 2 + 1 - h) for f in slots for h in (0, 1)]

    frame = jax.ShapeDtypeStruct((rows, 2 * half), BF16)
    half_frame = jax.ShapeDtypeStruct((rows, half), BF16)
    piece = jax.ShapeDtypeStruct((rows, group), BF16)
    pair = jax.ShapeDtypeStruct((2, rows, group), BF16)
    sums = jax.ShapeDtypeStruct((2, rows, group), F32)
    stats = jax.ShapeDtypeStruct((2, rows, HEAD_DIM), F32)

    def columns():
        return pl.BlockSpec((2 * half, group), lambda i, m, *_: (0, m[1]))

    def fresh_spec(step):
        return pl.BlockSpec((1, rows, half), lambda *_: (step, 0, 0))

    mine = latents[0]
    theirs = on_sides(mine)
    near_mine = on_queue(mine, near)
    far_mine = on_both(mine, far_open)

    (mod_mine,) = call(
        functools.partial(prepare_body, queue), [meta, level_index],
        [jnp.transpose(w_mod, (1, 0, 2))], [None],
        [jax.ShapeDtypeStruct((16, half), F32)],
    )
    mod_theirs = on_sides(mod_mine)
    near_mine, far_mine, theirs, mod_mine = tie(near_mine, far_mine, theirs, mod_mine)

    def normed(pairs, jobs):
        args = [x for p in pairs for x in p] + [mod_mine, mod_theirs]
        return call(
            functools.partial(norm_body, jobs), [meta], args, [None] * len(args),
            [frame] * len(pairs),
        )

    def local(step, own):
        other = [on_queue(x, core_swap) for x in own]
        return call(
            functools.partial(local_body, step, queue, len(own)), [meta, window_width],
            own + other + [w_query, w_key, w_value], [None] * 2 * len(own) + [columns()] * 3,
            [pair, sums, stats],
            scratch=[pltpu.VMEM((2, rows, group), BF16)] * 2,
            flops=2 * 2 * rows * 2 * half * 3 * group + 4 * 2 * rows * 2 * rows * group,
        )

    def halo(step, near_own, far_own, state, final):
        count = near_own.shape[0]
        near_own, far_own, *state = tie(near_own, far_own, *state)
        near_other = on_queue(near_own, core_swap)
        far_other = on_queue(far_own, core_swap)
        return call(
            functools.partial(halo_body, step, queue, final), [meta, window_width],
            [near_own, near_other, far_own, far_other, w_key, w_value] + state,
            [None] * 4 + [columns()] * 2 + [None] * 3,
            [piece, piece] if final else [sums, stats],
            scratch=[pltpu.VMEM((4, count, group), BF16)] * 2,
            flops=2 * 4 * count * 2 * half * 2 * group + 4 * 2 * rows * 3 * count * group,
        )

    def exchanged(m_own, m_other):
        return [
            m_own, on_queue(m_other, core_swap), on_sides(m_own),
            on_both(m_other, aside(lambda f: f ^ 1)),
        ]

    def w_specs(flip):
        col = (lambda m: 1 - m[0]) if flip else (lambda m: m[0])
        return [
            pl.BlockSpec((group, half), lambda i, m, *_: (m[1], col(m))),
            pl.BlockSpec((group, half), lambda i, m, *_: (1 - m[1], col(m))),
        ] + [
            pl.BlockSpec((n, half), lambda i, m, *_: (0, col(m))) for n in (wide, group - wide)
        ] * 2

    near_theirs = on_sides(near_mine)
    far_theirs = on_both(theirs, far_open)
    (own,) = normed([(mine, theirs)], [(0, False)])
    state = local(0, [own])
    near_theirs, far_theirs, *state = tie(near_theirs, far_theirs, *state)
    near_own, far_own = normed(
        [(near_mine, near_theirs), (far_mine, far_theirs)], [(1, False), (2, True)]
    )
    near_own, far_own, w_out_late = tie(near_own, far_own, w_out)
    send = call(
        copy_body, [meta], [w_out_late],
        [pl.BlockSpec((group, 2 * half), lambda i, m, *_: (m[1], 0))],
        [jax.ShapeDtypeStruct((n, 2 * half), BF16) for n in (wide, group - wide)],
    )
    far_weights = [on_both(send[0], aside(lambda f: f ^ chips)), on_sides(send[1])]
    fresh_theirs = on_both(fresh_noise[0], head_only)
    m_own, m_other = halo(0, near_own, far_own, state, True)
    mixed = exchanged(m_own, m_other)
    *far_weights, _, _ = tie(*far_weights, mixed[2], mixed[3])
    far_weights_other = [on_queue(w, core_swap) for w in far_weights]
    weights = [w_out, w_out, *far_weights, *far_weights_other]
    vel0, latent, own = call(
        out_step_body, [meta],
        mixed + weights * 2
        + [mine, theirs, fresh_noise, fresh_theirs, mod_mine, mod_theirs],
        [None] * 4 + w_specs(False) + w_specs(True) + [None, None, fresh_spec(0), None, None, None],
        [half_frame, half_frame, frame], flops=2 * rows * 4 * half * half,
    )

    near_own, far_own = on_queue(own, near), on_both(own, far_ring)
    state = local(1, [own])
    mixed = exchanged(*halo(1, near_own, far_own, state, True))
    vel1, upd1 = call(
        out_last_body, [meta], mixed + weights + [latent, fresh_noise, mod_mine],
        [None] * 4 + w_specs(False) + [None, fresh_spec(1), None],
        [half_frame, half_frame], flops=2 * rows * 2 * half * half,
    )
    latent = on_queue(upd1, [(f, (f - 2) % queue) for f in slots])
    vel1 = on_queue(vel1, [(f, (f - 1) % queue) for f in slots])
    return (latent[None], jnp.stack([vel0, vel1])[:, None])


def solution(mesh):
    in_specs = (
        P("queue", None, "heads"),
        P(None, None, "heads"),
        P(),
        P(),
        P(None, None, "heads"),
        P(None, "heads"),
        P(None, "heads"),
        P(None, "heads"),
        P("heads", None),
    )
    out_specs = (P("queue", None, "heads"), P(None, "queue", None, "heads"))
    return jax.shard_map(
        per_device, mesh=mesh, in_specs=in_specs, out_specs=out_specs, check_vma=False
    )
```

```python
import functools
import math

import jax
import jax.numpy as jnp
from jax import lax
from jax.experimental import pallas as pl
from jax.experimental.pallas import tpu as pltpu
from jax.sharding import PartitionSpec as P

HEAD_DIM = 128
STRIDE = 8
NORM_EPS = 1e-06
BF16 = jnp.bfloat16
F32 = jnp.float32
VMEM_LIMIT = 32 * 1024 * 1024
SCORE_FACTOR = math.log2(math.e) / math.sqrt(HEAD_DIM)
SLOTS = 5
SHIFT, SCALE, GATE, CHANGE = 0, SLOTS, 2 * SLOTS, 3 * SLOTS
TABLE_ROWS = 24


def dot(a, b):
    return jnp.dot(a, b, preferred_element_type=F32)


def whole(shape):
    return pl.BlockSpec(shape, functools.partial(lambda n, *_: (0,) * n, len(shape)))


def call(body, meta, args, specs, outs, scratch=(), room=VMEM_LIMIT):
    return pl.pallas_call(
        body,
        grid_spec=pltpu.PrefetchScalarGridSpec(
            num_scalar_prefetch=len(meta),
            grid=(1,),
            in_specs=[whole(a.shape) if s is None else s for a, s in zip(args, specs)],
            out_specs=[whole(o.shape) for o in outs],
            scratch_shapes=scratch,
        ),
        out_shape=outs,
        compiler_params=pltpu.CompilerParams(vmem_limit_bytes=room),
        cost_estimate=pl.CostEstimate(flops=1, bytes_accessed=1, transcendentals=0),
    )(*meta, *args)


def sigma_of(level, levels):
    share = level / levels
    return 5.0 * share / (1.0 + 4.0 * share)


def prepare_body(queue, meta_ref, level_ref, w_mod, mod_ref):
    place, behind = meta_ref[2], meta_ref[3]
    before = (place - 1) & (queue - 1)
    rows = lax.broadcasted_iota(jnp.int32, (16, w_mod.shape[1] // 2), 0)
    level = jnp.zeros(rows.shape, jnp.int32)
    for i, at in enumerate((place, place ^ 2, behind, before, place ^ 1)):
        level = jnp.where(rows == i, level_ref[at], level)
    freqs = w_mod.shape[1] // 2
    index_k = lax.broadcasted_iota(jnp.int32, (16, freqs), 1).astype(F32)
    phase = level.astype(F32) * jnp.exp(-math.log(10000.0) * index_k / freqs)
    low = jnp.cos(phase).astype(BF16)
    high = jnp.sin(phase).astype(BF16)
    for kind in range(3):
        table = dot(low, w_mod[kind, :freqs, :]) + dot(high, w_mod[kind, freqs:, :])
        mod_ref[SLOTS * kind : SLOTS * (kind + 1), :] = table[:SLOTS, :]
    levels = queue * STRIDE
    for i, slot in enumerate((place, before)):
        sigma = [
            sigma_of(jnp.full((1, mod_ref.shape[1]), level_ref[at], jnp.int32).astype(F32), levels)
            for at in (slot, (slot - 1) & (queue - 1))
        ]
        mod_ref[CHANGE + i : CHANGE + i + 1, :] = jnp.where(slot > 0, sigma[1], 0.0) - sigma[0]
    unused = TABLE_ROWS - CHANGE - 2
    mod_ref[CHANGE + 2 :, :] = jnp.zeros((unused, mod_ref.shape[1]), F32)


def pack_body(meta_ref, wq, wk, wv, w_rows, query_ref, pair_ref, wide_ref, narrow_ref):
    group = wk.shape[1]
    query_ref[...] = wq[...]
    pair_ref[:, :group] = wk[...]
    pair_ref[:, group:] = wv[...]
    wide = wide_ref.shape[0]
    wide_ref[...] = w_rows[:wide, :]
    narrow_ref[...] = w_rows[wide:, :]


def lane_block(index, width):
    return pl.ds(pl.multiple_of(index * width, HEAD_DIM), width)


def normalize(a, b, mod_a, mod_b, slot, side, out_ref):
    a = a.astype(F32)
    b = b.astype(F32)
    half = a.shape[1]
    width = 2 * half
    total = jnp.sum(a, axis=-1, keepdims=True) + jnp.sum(b, axis=-1, keepdims=True)
    square = jnp.sum(a * a, axis=-1, keepdims=True) + jnp.sum(b * b, axis=-1, keepdims=True)
    mean = total / width
    inv = lax.rsqrt(square / width - mean * mean + NORM_EPS)
    for x, mod, at in ((a, mod_a, side), (b, mod_b, 1 - side)):
        scale, shift = mod(SCALE + slot), mod(SHIFT + slot)
        out_ref[:, lane_block(at, half)] = (
            (x - mean) * inv * (1.0 + scale) + shift
        ).astype(BF16)


def norm_body(jobs, meta_ref, *refs):
    count = len(jobs)
    mod_m, mod_t = refs[2 * count : 2 * count + 2]
    for i, (slot, may_cross) in enumerate(jobs):
        side = meta_ref[0]
        row_m = lambda r: mod_m[r : r + 1, :]
        row_t = lambda r: mod_t[r : r + 1, :]
        if may_cross:
            crossed = meta_ref[4] == 1
            side = side ^ meta_ref[4]
            mod_a = lambda r: jnp.where(crossed, row_t(r), row_m(r))
            mod_b = lambda r: jnp.where(crossed, row_m(r), row_t(r))
        else:
            mod_a, mod_b = row_m, row_t
        normalize(
            refs[2 * i][...], refs[2 * i + 1][...], mod_a, mod_b, slot, side,
            refs[2 * count + 2 + i],
        )


def lane_max(scores, allowed):
    best = None
    for s, ok in zip(scores, allowed):
        top = s[:, :HEAD_DIM]
        for at in range(HEAD_DIM, s.shape[1], HEAD_DIM):
            top = jnp.maximum(top, s[:, at : at + HEAD_DIM])
        top = jnp.where(ok, top, -1e30)
        best = top if best is None else jnp.maximum(best, top)
    return jnp.max(best, axis=-1, keepdims=True)


def weigh(scores, allowed, top, values):
    total, mixed = None, None
    for s, ok, v in zip(scores, allowed, values):
        w = jnp.exp2(s - jnp.where(ok, top, 1e30))
        part = w[:, :HEAD_DIM]
        for at in range(HEAD_DIM, s.shape[1], HEAD_DIM):
            part = part + w[:, at : at + HEAD_DIM]
        total = part if total is None else total + part
        product = dot(w.astype(BF16), v)
        mixed = product if mixed is None else mixed + product
    return jnp.sum(total, axis=-1, keepdims=True), mixed


def scores_of(query, keys):
    return lax.dot_general(query, keys, (((1,), (1,)), ((), ())), preferred_element_type=F32)


def within(slot, offset, reach, queue):
    at = slot + offset
    return (jnp.abs(offset) <= reach) & (at >= 0) & (at < queue)


def local_body(step, queue, meta_ref, width_ref, *refs):
    if step == 0:
        own_m, own_t, other_m, other_t, mod_m, mod_t = refs[:6]
        wq, wkv, q_ref, acc_ref, stat_ref, ks, vs, normed = refs[6:]
        row_m = lambda r: mod_m[r : r + 1, :]
        row_t = lambda r: mod_t[r : r + 1, :]
        side = meta_ref[0]
        normalize(own_m[...], own_t[...], row_m, row_t, 0, side, normed.at[0])
        normalize(other_m[...], other_t[...], row_m, row_t, 4, side, normed.at[1])
        frames = normed.at[0], normed.at[1]
    else:
        frames = refs[:2]
        wq, wkv, q_ref, acc_ref, stat_ref, ks, vs = refs[2:]
    place = meta_ref[2]
    group = ks.shape[2]
    for i, frame in enumerate(frames):
        both = dot(frame[...], wkv[...])
        ks[i] = both[:, :group].astype(BF16)
        vs[i] = both[:, group:].astype(BF16)
        q_ref[i] = (dot(frame[...], wq[...]) * SCORE_FACTOR).astype(BF16)
    for qi in range(2):
        here = place ^ qi
        slot = (here - step) & (queue - 1)
        reach = width_ref[slot]
        aside = 1 - 2 * (here & 1)
        allowed = (reach >= 0, within(slot, aside, reach, queue))
        for head in range(ks.shape[2] // HEAD_DIM):
            lanes = slice(head * HEAD_DIM, (head + 1) * HEAD_DIM)
            query = q_ref[qi, :, lanes]
            scores = [scores_of(query, ks[j, :, lanes]) for j in (qi, 1 - qi)]
            top = lane_max(scores, allowed)
            total, mixed = weigh(scores, allowed, top, [vs[j, :, lanes] for j in (qi, 1 - qi)])
            acc_ref[qi, :, lanes] = mixed
            stat_ref[qi, :, head : head + 1] = top
            stat_ref[qi, :, 8 + head : 9 + head] = total


def halo_body(
    step, queue, meta_ref, width_ref,
    a_own, a_other, b_own, b_other, wkv, q_ref, acc_in, stat_in, own_out, other_out, ks, vs,
):
    group = ks.shape[2]
    place, behind = meta_ref[2], meta_ref[3]
    for i, frame in enumerate((a_own, a_other, b_own, b_other)):
        both = dot(frame[...], wkv[...])
        ks[i] = both[:, :group].astype(BF16)
        vs[i] = both[:, group:].astype(BF16)
    for qi, out in enumerate((own_out, other_out)):
        here = place ^ qi
        slot = (here - step) & (queue - 1)
        reach = width_ref[slot]
        index, allowed = [], []
        for offset in (-2, 2, 2 * (here & 1) - 1):
            there = (here + offset) & (queue - 1)
            pick = jnp.int32(3)
            for j, known in enumerate((place ^ 2, place ^ 3, behind)):
                pick = jnp.where(there == known, j, pick)
            index.append(pick)
            allowed.append(within(slot, jnp.int32(offset), reach, queue))
        for head in range(ks.shape[2] // HEAD_DIM):
            lanes = slice(head * HEAD_DIM, (head + 1) * HEAD_DIM)
            query = q_ref[qi, :, lanes]
            scores = [scores_of(query, ks[j, :, lanes]) for j in index]
            before = stat_in[qi, :, head : head + 1]
            top = jnp.maximum(before, lane_max(scores, allowed))
            total, mixed = weigh(scores, allowed, top, [vs[j, :, lanes] for j in index])
            fade = jnp.exp2(before - top)
            total = total + fade * stat_in[qi, :, 8 + head : 9 + head]
            mixed = mixed + fade * acc_in[qi, :, lanes]
            out[:, lanes] = (mixed / total).astype(BF16)


def output_sums(mixed, weights):
    m_self, m_core, m_y, m_yx = mixed
    w_self, w_core, w_y0, w_y1, w_x0, w_x1 = weights
    wide = w_y0.shape[0]
    sums = dot(m_self[...], w_self[...]) + dot(m_core[...], w_core[...])
    sums += dot(m_y[:, :wide], w_y0[...]) + dot(m_y[:, wide:], w_y1[...])
    return sums + dot(m_yx[:, :wide], w_x0[...]) + dot(m_yx[:, wide:], w_x1[...])


def out_step_body(
    meta_ref,
    m_self, m_core, m_y, m_yx, *rest,
):
    lat_m, lat_t, fresh_m, fresh_t, mod_m, mod_t, vel_ref, next_ref, normed_ref = rest[12:]
    mixed = m_self, m_core, m_y, m_yx
    change = mod_m[CHANGE : CHANGE + 1, :]
    first = meta_ref[2] == 0
    fresh = (fresh_m[0], fresh_t[...])
    nexts = []
    for side, (lat, mod) in enumerate(((lat_m, mod_m), (lat_t, mod_t))):
        proj = output_sums(mixed, rest[6 * side : 6 * side + 6])
        state = lat[...].astype(F32)
        velocity = state + mod[GATE : GATE + 1, :] * proj
        updated = (state + change * velocity).astype(BF16)
        if side == 0:
            vel_ref[...] = velocity.astype(BF16)
        nexts.append(jnp.where(first, fresh[side].astype(F32), updated.astype(F32)))
    next_ref[...] = nexts[0].astype(BF16)
    normalize(
        nexts[0], nexts[1], lambda r: mod_m[r : r + 1, :], lambda r: mod_t[r : r + 1, :],
        3, meta_ref[0], normed_ref,
    )


def out_last_body(
    meta_ref,
    m_self, m_core, m_y, m_yx, *rest,
):
    latent, fresh, mod_m, vel_ref, upd_ref = rest[6:]
    proj = output_sums((m_self, m_core, m_y, m_yx), rest[:6])
    state = latent[...].astype(F32)
    velocity = state + mod_m[GATE + 3 : GATE + 4, :] * proj
    vel_ref[...] = velocity.astype(BF16)
    updated = state + mod_m[CHANGE + 1 : CHANGE + 2, :] * velocity
    leaves = meta_ref[2] == 1
    upd_ref[...] = jnp.where(leaves, fresh[0].astype(F32), updated).astype(BF16)


def join_body(meta_ref, latent, first, second, latent_ref, both_ref):
    latent_ref[...] = latent[...]
    both_ref[0] = first[...]
    both_ref[1] = second[...]


def tie(*arrays):
    return lax.optimization_barrier(arrays)


def per_device(
    latents, fresh_noise, level_index, window_width, w_mod, w_query, w_key, w_value, w_out
):
    queue = lax.axis_size("queue")
    place = lax.axis_index("queue")
    side = lax.axis_index("heads")
    core = place & 1
    chips = queue // 2

    def behind_of(f):
        chip = f >> 1
        return (((chip + 1 if chip & 1 else chip - 1) % chips) << 1) | (f & 1)

    chip = place >> 1
    behind = ((jnp.where(chip & 1 == 1, chip + 1, chip - 1) & (chips - 1)) << 1) | core
    crossed = ((place ^ behind) // chips) & 1
    meta = jnp.stack(
        [side, core, place, behind, crossed]
    ).astype(jnp.int32)

    rows, half = latents.shape[1:]
    group = half // 2
    wide = group - HEAD_DIM
    slots = range(queue)

    core_swap = [(f, f ^ 1) for f in slots]
    near = [(f, f ^ 2) for f in slots]
    far_ring = [
        (f * 2 + h, behind_of(f) * 2 + (h ^ (((f ^ behind_of(f)) // chips) & 1)))
        for f in slots
        for h in (0, 1)
    ]
    far_open = [(s, d if abs(s // 2 - d // 2) <= 2 else s) for s, d in far_ring]
    head_only = [(s, s ^ 1 if s < 2 else s) for s in range(2 * queue)]
    both = ("queue", "heads")

    def on_queue(x, perm):
        return lax.ppermute(x, "queue", perm)

    def on_sides(x):
        return lax.ppermute(x, "heads", [(0, 1), (1, 0)])

    def on_both(x, perm):
        return lax.ppermute(x, both, perm)

    def aside(to):
        return [(f * 2 + h, to(f) * 2 + 1 - h) for f in slots for h in (0, 1)]

    frame = jax.ShapeDtypeStruct((rows, 2 * half), BF16)
    half_frame = jax.ShapeDtypeStruct((rows, half), BF16)
    piece = jax.ShapeDtypeStruct((rows, group), BF16)
    pair = jax.ShapeDtypeStruct((2, rows, group), BF16)
    sums = jax.ShapeDtypeStruct((2, rows, group), F32)
    stats = jax.ShapeDtypeStruct((2, rows, HEAD_DIM), F32)

    def columns():
        return pl.BlockSpec((2 * half, group), lambda i, m, *_: (0, m[1]))

    def fresh_spec(step):
        return pl.BlockSpec((1, rows, half), lambda *_: (step, 0, 0))

    mine = latents[0]
    theirs = on_sides(mine)
    near_mine = on_queue(mine, near)
    far_mine = on_both(mine, far_open)

    (mod_mine,) = call(
        functools.partial(prepare_body, queue), [meta, level_index],
        [jnp.transpose(w_mod, (1, 0, 2))], [None],
        [jax.ShapeDtypeStruct((TABLE_ROWS, half), F32)],
    )
    mod_theirs = on_sides(mod_mine)
    w_query, w_pair, *send = call(
        pack_body, [meta], [w_query, w_key, w_value, w_out],
        [columns()] * 3 + [pl.BlockSpec((group, 2 * half), lambda i, m, *_: (m[1], 0))],
        [
            jax.ShapeDtypeStruct((2 * half, n), BF16) for n in (group, 2 * group)
        ] + [
            jax.ShapeDtypeStruct((n, 2 * half), BF16) for n in (wide, group - wide)
        ],
        room=58 * 1024 * 1024,
    )
    other_mine = on_queue(mine, core_swap)
    near_mine, far_mine, theirs, mod_mine, w_query, w_pair = tie(
        near_mine, far_mine, theirs, mod_mine, w_query, w_pair
    )
    other_theirs = on_queue(theirs, core_swap)

    def normed(pairs, jobs):
        args = [x for p in pairs for x in p] + [mod_mine, mod_theirs]
        return call(
            functools.partial(norm_body, jobs), [meta], args, [None] * len(args),
            [frame] * len(pairs),
        )

    def local(step, frames):
        scratch = [pltpu.VMEM((2, rows, group), BF16)] * 2
        if step == 0:
            scratch.append(pltpu.VMEM((2, rows, 2 * half), BF16))
        args = frames + [w_query, w_pair]
        return call(
            functools.partial(local_body, step, queue), [meta, window_width], args,
            [None] * len(args), [pair, sums, stats], scratch=scratch,
        )

    def halo(step, near_own, far_own, state):
        near_own, far_own, *state = tie(near_own, far_own, *state)
        near_other = on_queue(near_own, core_swap)
        far_other = on_queue(far_own, core_swap)
        args = [near_own, near_other, far_own, far_other, w_pair] + state
        return call(
            functools.partial(halo_body, step, queue), [meta, window_width], args,
            [None] * len(args), [piece, piece],
            scratch=[pltpu.VMEM((4, rows, group), BF16)] * 2,
        )

    def exchanged(m_own, m_other):
        return [
            m_own, on_queue(m_other, core_swap), on_sides(m_own),
            on_both(m_other, aside(lambda f: f ^ 1)),
        ]

    def w_specs(flip):
        col = (lambda m: 1 - m[0]) if flip else (lambda m: m[0])
        return [
            pl.BlockSpec((group, half), lambda i, m, *_: (m[1], col(m))),
            pl.BlockSpec((group, half), lambda i, m, *_: (1 - m[1], col(m))),
        ] + [
            pl.BlockSpec((n, half), lambda i, m, *_: (0, col(m))) for n in (wide, group - wide)
        ] * 2

    near_theirs = on_sides(near_mine)
    far_theirs = on_both(theirs, far_open)
    state = local(0, [mine, theirs, other_mine, other_theirs, mod_mine, mod_theirs])
    fresh_theirs = on_both(fresh_noise[0], head_only)
    near_theirs, far_theirs, fresh_theirs, *state = tie(
        near_theirs, far_theirs, fresh_theirs, *state
    )
    near_own, far_own = normed(
        [(near_mine, near_theirs), (far_mine, far_theirs)], [(1, False), (2, True)]
    )
    near_own, far_own, *send = tie(near_own, far_own, *send)
    far_weights = [on_both(send[0], aside(lambda f: f ^ chips)), on_sides(send[1])]
    m_own, m_other = halo(0, near_own, far_own, state)
    mixed = exchanged(m_own, m_other)
    *far_weights, _, _ = tie(*far_weights, mixed[2], mixed[3])
    far_weights_other = [on_queue(w, core_swap) for w in far_weights]
    weights = [w_out, w_out, *far_weights, *far_weights_other]
    vel0, latent, own = call(
        out_step_body, [meta],
        mixed + weights * 2
        + [mine, theirs, fresh_noise, fresh_theirs, mod_mine, mod_theirs],
        [None] * 4 + w_specs(False) + w_specs(True) + [None, None, fresh_spec(0), None, None, None],
        [half_frame, half_frame, frame],
    )

    near_own, far_own = on_queue(own, near), on_both(own, far_ring)
    state = local(1, [own, on_queue(own, core_swap)])
    mixed = exchanged(*halo(1, near_own, far_own, state))
    vel1, upd1 = call(
        out_last_body, [meta], mixed + weights + [latent, fresh_noise, mod_mine],
        [None] * 4 + w_specs(False) + [None, fresh_spec(1), None],
        [half_frame, half_frame],
    )
    latent = on_queue(upd1, [(f, (f - 2) % queue) for f in slots])
    vel1 = on_queue(vel1, [(f, (f - 1) % queue) for f in slots])
    latent, velocities = call(
        join_body, [meta], [latent, vel0, vel1], [None] * 3,
        [half_frame, jax.ShapeDtypeStruct((2, rows, half), BF16)],
    )
    return (latent[None], velocities[:, None])


def solution(mesh):
    in_specs = (
        P("queue", None, "heads"),
        P(None, None, "heads"),
        P(),
        P(),
        P(None, None, "heads"),
        P(None, "heads"),
        P(None, "heads"),
        P(None, "heads"),
        P("heads", None),
    )
    out_specs = (P("queue", None, "heads"), P(None, "queue", None, "heads"))
    return jax.shard_map(
        per_device, mesh=mesh, in_specs=in_specs, out_specs=out_specs, check_vma=False
    )
```

```python
import functools
import math

import jax
import jax.numpy as jnp
from jax import lax
from jax.experimental import pallas as pl
from jax.experimental.pallas import tpu as pltpu
from jax.sharding import PartitionSpec as P

HEAD_DIM = 128
STRIDE = 8
NORM_EPS = 1e-06
BF16 = jnp.bfloat16
F32 = jnp.float32
VMEM_LIMIT = 32 * 1024 * 1024
SCORE_FACTOR = math.log2(math.e) / math.sqrt(HEAD_DIM)
SLOTS = 5
SHIFT, SCALE, GATE, CHANGE = 0, SLOTS, 2 * SLOTS, 3 * SLOTS
TABLE_ROWS = 24


def dot(a, b):
    return jnp.dot(a, b, preferred_element_type=F32)


def whole(shape):
    return pl.BlockSpec(shape, functools.partial(lambda n, *_: (0,) * n, len(shape)))


def call(body, meta, args, specs, outs, scratch=(), room=VMEM_LIMIT):
    return pl.pallas_call(
        body,
        grid_spec=pltpu.PrefetchScalarGridSpec(
            num_scalar_prefetch=len(meta),
            grid=(1,),
            in_specs=[whole(a.shape) if s is None else s for a, s in zip(args, specs)],
            out_specs=[whole(o.shape) for o in outs],
            scratch_shapes=scratch,
        ),
        out_shape=outs,
        compiler_params=pltpu.CompilerParams(vmem_limit_bytes=room),
        cost_estimate=pl.CostEstimate(flops=1, bytes_accessed=1, transcendentals=0),
    )(*meta, *args)


def sigma_of(level, levels):
    share = level / levels
    return 5.0 * share / (1.0 + 4.0 * share)


def prepare_body(queue, meta_ref, level_ref, w_mod, mod_ref):
    place, behind = meta_ref[2], meta_ref[3]
    before = (place - 1) & (queue - 1)
    rows = lax.broadcasted_iota(jnp.int32, (16, w_mod.shape[1] // 2), 0)
    level = jnp.zeros(rows.shape, jnp.int32)
    for i, at in enumerate((place, place ^ 2, behind, before, place ^ 1)):
        level = jnp.where(rows == i, level_ref[at], level)
    freqs = w_mod.shape[1] // 2
    index_k = lax.broadcasted_iota(jnp.int32, (16, freqs), 1).astype(F32)
    phase = level.astype(F32) * jnp.exp(-math.log(10000.0) * index_k / freqs)
    low = jnp.cos(phase).astype(BF16)
    high = jnp.sin(phase).astype(BF16)
    for kind in range(3):
        table = dot(low, w_mod[kind, :freqs, :]) + dot(high, w_mod[kind, freqs:, :])
        mod_ref[SLOTS * kind : SLOTS * (kind + 1), :] = table[:SLOTS, :]
    levels = queue * STRIDE
    for i, slot in enumerate((place, before)):
        sigma = [
            sigma_of(jnp.full((1, mod_ref.shape[1]), level_ref[at], jnp.int32).astype(F32), levels)
            for at in (slot, (slot - 1) & (queue - 1))
        ]
        mod_ref[CHANGE + i : CHANGE + i + 1, :] = jnp.where(slot > 0, sigma[1], 0.0) - sigma[0]
    unused = TABLE_ROWS - CHANGE - 2
    mod_ref[CHANGE + 2 :, :] = jnp.zeros((unused, mod_ref.shape[1]), F32)


def pack_body(meta_ref, wq, wk, wv, w_rows, query_ref, pair_ref, wide_ref, narrow_ref):
    group = wk.shape[1]
    query_ref[...] = wq[...]
    pair_ref[:, :group] = wk[...]
    pair_ref[:, group:] = wv[...]
    wide = wide_ref.shape[0]
    wide_ref[...] = w_rows[:wide, :]
    narrow_ref[...] = w_rows[wide:, :]


def lane_block(index, width):
    return pl.ds(pl.multiple_of(index * width, HEAD_DIM), width)


def normalize(a, b, mod_a, mod_b, slot, side, out_ref):
    a = a.astype(F32)
    b = b.astype(F32)
    half = a.shape[1]
    width = 2 * half
    total = jnp.sum(a, axis=-1, keepdims=True) + jnp.sum(b, axis=-1, keepdims=True)
    square = jnp.sum(a * a, axis=-1, keepdims=True) + jnp.sum(b * b, axis=-1, keepdims=True)
    mean = total / width
    inv = lax.rsqrt(square / width - mean * mean + NORM_EPS)
    for x, mod, at in ((a, mod_a, side), (b, mod_b, 1 - side)):
        scale, shift = mod(SCALE + slot), mod(SHIFT + slot)
        out_ref[:, lane_block(at, half)] = (
            (x - mean) * inv * (1.0 + scale) + shift
        ).astype(BF16)


def norm_body(jobs, meta_ref, *refs):
    count = len(jobs)
    mod_m, mod_t = refs[2 * count : 2 * count + 2]
    for i, (slot, may_cross) in enumerate(jobs):
        side = meta_ref[0]
        row_m = lambda r: mod_m[r : r + 1, :]
        row_t = lambda r: mod_t[r : r + 1, :]
        if may_cross:
            crossed = meta_ref[4] == 1
            side = side ^ meta_ref[4]
            mod_a = lambda r: jnp.where(crossed, row_t(r), row_m(r))
            mod_b = lambda r: jnp.where(crossed, row_m(r), row_t(r))
        else:
            mod_a, mod_b = row_m, row_t
        normalize(
            refs[2 * i][...], refs[2 * i + 1][...], mod_a, mod_b, slot, side,
            refs[2 * count + 2 + i],
        )


def lane_max(scores, allowed):
    best = None
    for s, ok in zip(scores, allowed):
        top = s[:, :HEAD_DIM]
        for at in range(HEAD_DIM, s.shape[1], HEAD_DIM):
            top = jnp.maximum(top, s[:, at : at + HEAD_DIM])
        top = jnp.where(ok, top, -1e30)
        best = top if best is None else jnp.maximum(best, top)
    return jnp.max(best, axis=-1, keepdims=True)


def weigh(scores, allowed, top, values):
    total, mixed = None, None
    for s, ok, v in zip(scores, allowed, values):
        w = jnp.exp2(s - jnp.where(ok, top, 1e30))
        part = w[:, :HEAD_DIM]
        for at in range(HEAD_DIM, s.shape[1], HEAD_DIM):
            part = part + w[:, at : at + HEAD_DIM]
        total = part if total is None else total + part
        product = dot(w.astype(BF16), v)
        mixed = product if mixed is None else mixed + product
    return jnp.sum(total, axis=-1, keepdims=True), mixed


def scores_of(query, keys):
    return lax.dot_general(query, keys, (((1,), (1,)), ((), ())), preferred_element_type=F32)


def within(slot, offset, reach, queue):
    at = slot + offset
    return (jnp.abs(offset) <= reach) & (at >= 0) & (at < queue)


def first_local_body(
    queue, meta_ref, width_ref, own_m, own_t, other_m, other_t, mod_m, mod_t, wq, wkv,
    q_ref, acc_ref, stat_ref, kv_ref, normed,
):
    row_m = lambda r: mod_m[r : r + 1, :]
    row_t = lambda r: mod_t[r : r + 1, :]
    side = meta_ref[0]
    normalize(own_m[...], own_t[...], row_m, row_t, 0, side, normed.at[0])
    normalize(other_m[...], other_t[...], row_m, row_t, 4, side, normed.at[1])
    project_body(meta_ref, normed.at[0], normed.at[1], wq, wkv, q_ref, kv_ref)
    local_body(0, queue, meta_ref, width_ref, q_ref, kv_ref, acc_ref, stat_ref)


def project_body(meta_ref, own, other, wq, wkv, q_ref, kv_ref):
    for i, frame in enumerate((own, other)):
        kv_ref[i] = dot(frame[...], wkv[...]).astype(BF16)
        q_ref[i] = (dot(frame[...], wq[...]) * SCORE_FACTOR).astype(BF16)


def local_body(step, queue, meta_ref, width_ref, q_ref, kv_ref, acc_ref, stat_ref):
    place = meta_ref[2]
    group = kv_ref.shape[2] // 2
    for qi in range(2):
        here = place ^ qi
        slot = (here - step) & (queue - 1)
        reach = width_ref[slot]
        aside = 1 - 2 * (here & 1)
        allowed = (reach >= 0, within(slot, aside, reach, queue))
        for head in range(group // HEAD_DIM):
            lanes = slice(head * HEAD_DIM, (head + 1) * HEAD_DIM)
            value_lanes = slice(group + head * HEAD_DIM, group + (head + 1) * HEAD_DIM)
            query = q_ref[qi, :, lanes]
            scores = [scores_of(query, kv_ref[j, :, lanes]) for j in (qi, 1 - qi)]
            top = lane_max(scores, allowed)
            values = [kv_ref[j, :, value_lanes] for j in (qi, 1 - qi)]
            total, mixed = weigh(scores, allowed, top, values)
            acc_ref[qi, :, lanes] = mixed
            stat_ref[qi, :, head : head + 1] = top
            stat_ref[qi, :, 8 + head : 9 + head] = total


def halo_body(
    step, queue, meta_ref, width_ref, *refs
):
    sources, (q_ref, acc_in, stat_in, own_out, other_out, ks, vs) = refs[:-7], refs[-7:]
    group = ks.shape[2]
    place, behind = meta_ref[2], meta_ref[3]
    if step == 0:
        *frames, wkv = sources
        for i, frame in enumerate(frames):
            both = dot(frame[...], wkv[...])
            ks[i] = both[:, :group].astype(BF16)
            vs[i] = both[:, group:].astype(BF16)
    else:
        for i in range(4):
            ks[i] = sources[i // 2][i % 2, :, :group]
            vs[i] = sources[i // 2][i % 2, :, group:]
    for qi, out in enumerate((own_out, other_out)):
        here = place ^ qi
        slot = (here - step) & (queue - 1)
        reach = width_ref[slot]
        index, allowed = [], []
        for offset in (-2, 2, 2 * (here & 1) - 1):
            there = (here + offset) & (queue - 1)
            pick = jnp.int32(3)
            for j, known in enumerate((place ^ 2, place ^ 3, behind)):
                pick = jnp.where(there == known, j, pick)
            index.append(pick)
            allowed.append(within(slot, jnp.int32(offset), reach, queue))
        for head in range(ks.shape[2] // HEAD_DIM):
            lanes = slice(head * HEAD_DIM, (head + 1) * HEAD_DIM)
            query = q_ref[qi, :, lanes]
            scores = [scores_of(query, ks[j, :, lanes]) for j in index]
            before = stat_in[qi, :, head : head + 1]
            top = jnp.maximum(before, lane_max(scores, allowed))
            total, mixed = weigh(scores, allowed, top, [vs[j, :, lanes] for j in index])
            fade = jnp.exp2(before - top)
            total = total + fade * stat_in[qi, :, 8 + head : 9 + head]
            mixed = mixed + fade * acc_in[qi, :, lanes]
            out[:, lanes] = (mixed / total).astype(BF16)


def output_sums(mixed, weights):
    m_self, m_core, m_y, m_yx = mixed
    w_self, w_core, w_y0, w_y1, w_x0, w_x1 = weights
    wide = w_y0.shape[0]
    sums = dot(m_self[...], w_self[...]) + dot(m_core[...], w_core[...])
    sums += dot(m_y[:, :wide], w_y0[...]) + dot(m_y[:, wide:], w_y1[...])
    return sums + dot(m_yx[:, :wide], w_x0[...]) + dot(m_yx[:, wide:], w_x1[...])


def out_step_body(
    meta_ref,
    m_self, m_core, m_y, m_yx, *rest,
):
    lat_m, lat_t, fresh_m, fresh_t, mod_m, mod_t, vel_ref, next_ref, normed_ref = rest[12:]
    mixed = m_self, m_core, m_y, m_yx
    change = mod_m[CHANGE : CHANGE + 1, :]
    first = meta_ref[2] == 0
    fresh = (fresh_m[0], fresh_t[...])
    nexts = []
    for side, (lat, mod) in enumerate(((lat_m, mod_m), (lat_t, mod_t))):
        proj = output_sums(mixed, rest[6 * side : 6 * side + 6])
        state = lat[...].astype(F32)
        velocity = state + mod[GATE : GATE + 1, :] * proj
        updated = (state + change * velocity).astype(BF16)
        if side == 0:
            vel_ref[...] = velocity.astype(BF16)
        nexts.append(jnp.where(first, fresh[side].astype(F32), updated.astype(F32)))
    next_ref[...] = nexts[0].astype(BF16)
    normalize(
        nexts[0], nexts[1], lambda r: mod_m[r : r + 1, :], lambda r: mod_t[r : r + 1, :],
        3, meta_ref[0], normed_ref,
    )


def out_last_body(
    meta_ref,
    m_self, m_core, m_y, m_yx, *rest,
):
    latent, fresh, mod_m, vel_ref, upd_ref = rest[6:]
    proj = output_sums((m_self, m_core, m_y, m_yx), rest[:6])
    state = latent[...].astype(F32)
    velocity = state + mod_m[GATE + 3 : GATE + 4, :] * proj
    vel_ref[...] = velocity.astype(BF16)
    updated = state + mod_m[CHANGE + 1 : CHANGE + 2, :] * velocity
    leaves = meta_ref[2] == 1
    upd_ref[...] = jnp.where(leaves, fresh[0].astype(F32), updated).astype(BF16)


def join_body(meta_ref, latent, first, second, latent_ref, both_ref):
    latent_ref[...] = latent[...]
    both_ref[0] = first[...]
    both_ref[1] = second[...]


def tie(*arrays):
    return lax.optimization_barrier(arrays)


def per_device(
    latents, fresh_noise, level_index, window_width, w_mod, w_query, w_key, w_value, w_out
):
    queue = lax.axis_size("queue")
    place = lax.axis_index("queue")
    side = lax.axis_index("heads")
    core = place & 1
    chips = queue // 2

    def behind_of(f):
        chip = f >> 1
        return (((chip + 1 if chip & 1 else chip - 1) % chips) << 1) | (f & 1)

    chip = place >> 1
    behind = ((jnp.where(chip & 1 == 1, chip + 1, chip - 1) & (chips - 1)) << 1) | core
    crossed = ((place ^ behind) // chips) & 1
    meta = jnp.stack(
        [side, core, place, behind, crossed]
    ).astype(jnp.int32)

    rows, half = latents.shape[1:]
    group = half // 2
    wide = group - HEAD_DIM
    slots = range(queue)

    core_swap = [(f, f ^ 1) for f in slots]
    near = [(f, f ^ 2) for f in slots]
    far_ring = [
        (f * 2 + h, behind_of(f) * 2 + (h ^ (((f ^ behind_of(f)) // chips) & 1)))
        for f in slots
        for h in (0, 1)
    ]
    far_open = [(s, d if abs(s // 2 - d // 2) <= 2 else s) for s, d in far_ring]
    head_only = [(s, s ^ 1 if s < 2 else s) for s in range(2 * queue)]
    both = ("queue", "heads")

    def on_queue(x, perm):
        return lax.ppermute(x, "queue", perm)

    def on_sides(x):
        return lax.ppermute(x, "heads", [(0, 1), (1, 0)])

    def on_both(x, perm):
        return lax.ppermute(x, both, perm)

    def aside(to):
        return [(f * 2 + h, to(f) * 2 + 1 - h) for f in slots for h in (0, 1)]

    frame = jax.ShapeDtypeStruct((rows, 2 * half), BF16)
    half_frame = jax.ShapeDtypeStruct((rows, half), BF16)
    piece = jax.ShapeDtypeStruct((rows, group), BF16)
    pair = jax.ShapeDtypeStruct((2, rows, group), BF16)
    sums = jax.ShapeDtypeStruct((2, rows, group), F32)
    stats = jax.ShapeDtypeStruct((2, rows, HEAD_DIM), F32)

    def columns():
        return pl.BlockSpec((2 * half, group), lambda i, m, *_: (0, m[1]))

    def fresh_spec(step):
        return pl.BlockSpec((1, rows, half), lambda *_: (step, 0, 0))

    mine = latents[0]
    theirs = on_sides(mine)
    near_mine = on_queue(mine, near)
    far_mine = on_both(mine, far_open)

    (mod_mine,) = call(
        functools.partial(prepare_body, queue), [meta, level_index],
        [jnp.transpose(w_mod, (1, 0, 2))], [None],
        [jax.ShapeDtypeStruct((TABLE_ROWS, half), F32)],
    )
    mod_theirs = on_sides(mod_mine)
    w_query, w_pair, *send = call(
        pack_body, [meta], [w_query, w_key, w_value, w_out],
        [columns()] * 3 + [pl.BlockSpec((group, 2 * half), lambda i, m, *_: (m[1], 0))],
        [
            jax.ShapeDtypeStruct((2 * half, n), BF16) for n in (group, 2 * group)
        ] + [
            jax.ShapeDtypeStruct((n, 2 * half), BF16) for n in (wide, group - wide)
        ],
        room=58 * 1024 * 1024,
    )
    other_mine = on_queue(mine, core_swap)
    near_mine, far_mine, theirs, mod_mine, w_query, w_pair = tie(
        near_mine, far_mine, theirs, mod_mine, w_query, w_pair
    )
    other_theirs = on_queue(theirs, core_swap)

    def normed(pairs, jobs):
        args = [x for p in pairs for x in p] + [mod_mine, mod_theirs]
        return call(
            functools.partial(norm_body, jobs), [meta], args, [None] * len(args),
            [frame] * len(pairs),
        )

    def halo(step, sources, state):
        args = sources + state
        return call(
            functools.partial(halo_body, step, queue), [meta, window_width], args,
            [None] * len(args), [piece, piece],
            scratch=[pltpu.VMEM((4, rows, group), BF16)] * 2,
        )

    def exchanged(m_own, m_other):
        return [
            m_own, on_queue(m_other, core_swap), on_sides(m_own),
            on_both(m_other, aside(lambda f: f ^ 1)),
        ]

    def w_specs(flip):
        col = (lambda m: 1 - m[0]) if flip else (lambda m: m[0])
        return [
            pl.BlockSpec((group, half), lambda i, m, *_: (m[1], col(m))),
            pl.BlockSpec((group, half), lambda i, m, *_: (1 - m[1], col(m))),
        ] + [
            pl.BlockSpec((n, half), lambda i, m, *_: (0, col(m))) for n in (wide, group - wide)
        ] * 2

    near_theirs = on_sides(near_mine)
    far_theirs = on_both(theirs, far_open)
    state = call(
        functools.partial(first_local_body, queue), [meta, window_width],
        [mine, theirs, other_mine, other_theirs, mod_mine, mod_theirs, w_query, w_pair],
        [None] * 8, [pair, sums, stats],
        scratch=[
            pltpu.VMEM((2, rows, 2 * group), BF16), pltpu.VMEM((2, rows, 2 * half), BF16)
        ],
    )
    fresh_theirs = on_both(fresh_noise[0], head_only)
    near_theirs, far_theirs, fresh_theirs, *state = tie(
        near_theirs, far_theirs, fresh_theirs, *state
    )
    near_own, far_own = normed(
        [(near_mine, near_theirs), (far_mine, far_theirs)], [(1, False), (2, True)]
    )
    near_own, far_own, *send = tie(near_own, far_own, *send)
    far_weights = [on_both(send[0], aside(lambda f: f ^ chips)), on_sides(send[1])]
    near_own, far_own, *state = tie(near_own, far_own, *state)
    near_other = on_queue(near_own, core_swap)
    far_other = on_queue(far_own, core_swap)
    m_own, m_other = halo(0, [near_own, near_other, far_own, far_other, w_pair], state)
    mixed = exchanged(m_own, m_other)
    *far_weights, _, _ = tie(*far_weights, mixed[2], mixed[3])
    far_weights_other = [on_queue(w, core_swap) for w in far_weights]
    weights = [w_out, w_out, *far_weights, *far_weights_other]
    vel0, latent, own = call(
        out_step_body, [meta],
        mixed + weights * 2
        + [mine, theirs, fresh_noise, fresh_theirs, mod_mine, mod_theirs],
        [None] * 4 + w_specs(False) + w_specs(True) + [None, None, fresh_spec(0), None, None, None],
        [half_frame, half_frame, frame],
    )

    query, keyed = call(
        project_body, [meta], [own, on_queue(own, core_swap), w_query, w_pair], [None] * 4,
        [pair, jax.ShapeDtypeStruct((2, rows, 2 * group), BF16)],
    )
    near_keyed = on_queue(keyed, near)
    far_keyed = on_queue(keyed, [(f, behind_of(f)) for f in slots])
    sums0, stats0 = call(
        functools.partial(local_body, 1, queue), [meta, window_width], [query, keyed],
        [None] * 2, [sums, stats],
    )
    mixed = exchanged(*halo(1, [near_keyed, far_keyed], [query, sums0, stats0]))
    vel1, upd1 = call(
        out_last_body, [meta], mixed + weights + [latent, fresh_noise, mod_mine],
        [None] * 4 + w_specs(False) + [None, fresh_spec(1), None],
        [half_frame, half_frame],
    )
    latent = on_queue(upd1, [(f, (f - 2) % queue) for f in slots])
    vel1 = on_queue(vel1, [(f, (f - 1) % queue) for f in slots])
    latent, velocities = call(
        join_body, [meta], [latent, vel0, vel1], [None] * 3,
        [half_frame, jax.ShapeDtypeStruct((2, rows, half), BF16)],
    )
    return (latent[None], velocities[:, None])


def solution(mesh):
    in_specs = (
        P("queue", None, "heads"),
        P(None, None, "heads"),
        P(),
        P(),
        P(None, None, "heads"),
        P(None, "heads"),
        P(None, "heads"),
        P(None, "heads"),
        P("heads", None),
    )
    out_specs = (P("queue", None, "heads"), P(None, "queue", None, "heads"))
    return jax.shard_map(
        per_device, mesh=mesh, in_specs=in_specs, out_specs=out_specs, check_vma=False
    )
```

```python
import functools
import math

import jax
import jax.numpy as jnp
from jax import lax
from jax.experimental import pallas as pl
from jax.experimental.pallas import tpu as pltpu
from jax.sharding import PartitionSpec as P

HEAD_DIM = 128
STRIDE = 8
NORM_EPS = 1e-06
BF16 = jnp.bfloat16
F32 = jnp.float32
VMEM_LIMIT = 32 * 1024 * 1024
SCORE_FACTOR = math.log2(math.e) / math.sqrt(HEAD_DIM)
SLOTS = 5
SHIFT, SCALE, GATE, CHANGE = 0, SLOTS, 2 * SLOTS, 3 * SLOTS
TABLE_ROWS = 24


def dot(a, b):
    return jnp.dot(a, b, preferred_element_type=F32)


def whole(shape):
    return pl.BlockSpec(shape, functools.partial(lambda n, *_: (0,) * n, len(shape)))


def call(body, meta, args, specs, outs, scratch=(), room=VMEM_LIMIT):
    return pl.pallas_call(
        body,
        grid_spec=pltpu.PrefetchScalarGridSpec(
            num_scalar_prefetch=len(meta),
            grid=(1,),
            in_specs=[whole(a.shape) if s is None else s for a, s in zip(args, specs)],
            out_specs=[whole(o.shape) for o in outs],
            scratch_shapes=scratch,
        ),
        out_shape=outs,
        compiler_params=pltpu.CompilerParams(vmem_limit_bytes=room),
        cost_estimate=pl.CostEstimate(flops=1, bytes_accessed=1, transcendentals=0),
    )(*meta, *args)


def sigma_of(level, levels):
    share = level / levels
    return 5.0 * share / (1.0 + 4.0 * share)


def prepare_body(queue, meta_ref, level_ref, w_mod, mod_ref):
    place, behind = meta_ref[2], meta_ref[3]
    before = (place - 1) & (queue - 1)
    rows = lax.broadcasted_iota(jnp.int32, (16, w_mod.shape[1] // 2), 0)
    level = jnp.zeros(rows.shape, jnp.int32)
    for i, at in enumerate((place, place ^ 2, behind, before, place ^ 1)):
        level = jnp.where(rows == i, level_ref[at], level)
    freqs = w_mod.shape[1] // 2
    index_k = lax.broadcasted_iota(jnp.int32, (16, freqs), 1).astype(F32)
    phase = level.astype(F32) * jnp.exp(-math.log(10000.0) * index_k / freqs)
    low = jnp.cos(phase).astype(BF16)
    high = jnp.sin(phase).astype(BF16)
    for kind in range(3):
        table = dot(low, w_mod[kind, :freqs, :]) + dot(high, w_mod[kind, freqs:, :])
        mod_ref[SLOTS * kind : SLOTS * (kind + 1), :] = table[:SLOTS, :]
    levels = queue * STRIDE
    for i, slot in enumerate((place, before)):
        sigma = [
            sigma_of(jnp.full((1, mod_ref.shape[1]), level_ref[at], jnp.int32).astype(F32), levels)
            for at in (slot, (slot - 1) & (queue - 1))
        ]
        mod_ref[CHANGE + i : CHANGE + i + 1, :] = jnp.where(slot > 0, sigma[1], 0.0) - sigma[0]
    unused = TABLE_ROWS - CHANGE - 2
    mod_ref[CHANGE + 2 :, :] = jnp.zeros((unused, mod_ref.shape[1]), F32)


def pack_body(meta_ref, wq, wk, wv, w_rows, query_ref, pair_ref, wide_ref, narrow_ref):
    group = wk.shape[1]
    query_ref[...] = wq[...]
    pair_ref[:, :group] = wk[...]
    pair_ref[:, group:] = wv[...]
    wide = wide_ref.shape[0]
    wide_ref[...] = w_rows[:wide, :]
    narrow_ref[...] = w_rows[wide:, :]


def lane_block(index, width):
    return pl.ds(pl.multiple_of(index * width, HEAD_DIM), width)


def normalize(a, b, mod_a, mod_b, slot, side, out_ref):
    a = a.astype(F32)
    b = b.astype(F32)
    half = a.shape[1]
    width = 2 * half
    total = jnp.sum(a, axis=-1, keepdims=True) + jnp.sum(b, axis=-1, keepdims=True)
    square = jnp.sum(a * a, axis=-1, keepdims=True) + jnp.sum(b * b, axis=-1, keepdims=True)
    mean = total / width
    inv = lax.rsqrt(square / width - mean * mean + NORM_EPS)
    for x, mod, at in ((a, mod_a, side), (b, mod_b, 1 - side)):
        scale, shift = mod(SCALE + slot), mod(SHIFT + slot)
        out_ref[:, lane_block(at, half)] = (
            (x - mean) * inv * (1.0 + scale) + shift
        ).astype(BF16)


def norm_body(jobs, meta_ref, *refs):
    count = len(jobs)
    mod_m, mod_t = refs[2 * count : 2 * count + 2]
    for i, (slot, may_cross) in enumerate(jobs):
        side = meta_ref[0]
        row_m = lambda r: mod_m[r : r + 1, :]
        row_t = lambda r: mod_t[r : r + 1, :]
        if may_cross:
            crossed = meta_ref[4] == 1
            side = side ^ meta_ref[4]
            mod_a = lambda r: jnp.where(crossed, row_t(r), row_m(r))
            mod_b = lambda r: jnp.where(crossed, row_m(r), row_t(r))
        else:
            mod_a, mod_b = row_m, row_t
        normalize(
            refs[2 * i][...], refs[2 * i + 1][...], mod_a, mod_b, slot, side,
            refs[2 * count + 2 + i],
        )


def lane_max(scores, allowed):
    best = None
    for s, ok in zip(scores, allowed):
        top = s[:, :HEAD_DIM]
        for at in range(HEAD_DIM, s.shape[1], HEAD_DIM):
            top = jnp.maximum(top, s[:, at : at + HEAD_DIM])
        top = jnp.where(ok, top, -1e30)
        best = top if best is None else jnp.maximum(best, top)
    return jnp.max(best, axis=-1, keepdims=True)


def weigh(scores, allowed, top, values):
    total, mixed = None, None
    for s, ok, v in zip(scores, allowed, values):
        w = jnp.exp2(s - jnp.where(ok, top, 1e30))
        part = w[:, :HEAD_DIM]
        for at in range(HEAD_DIM, s.shape[1], HEAD_DIM):
            part = part + w[:, at : at + HEAD_DIM]
        total = part if total is None else total + part
        product = dot(w.astype(BF16), v)
        mixed = product if mixed is None else mixed + product
    return jnp.sum(total, axis=-1, keepdims=True), mixed


def scores_of(query, keys):
    return lax.dot_general(query, keys, (((1,), (1,)), ((), ())), preferred_element_type=F32)


def within(slot, offset, reach, queue):
    at = slot + offset
    return (jnp.abs(offset) <= reach) & (at >= 0) & (at < queue)


def first_local_body(
    queue, meta_ref, width_ref, own_m, own_t, other_m, other_t, mod_m, mod_t, wq, wkv,
    q_ref, acc_ref, stat_ref, kv_ref, normed,
):
    row_m = lambda r: mod_m[r : r + 1, :]
    row_t = lambda r: mod_t[r : r + 1, :]
    side = meta_ref[0]
    normalize(own_m[...], own_t[...], row_m, row_t, 0, side, normed.at[0])
    normalize(other_m[...], other_t[...], row_m, row_t, 4, side, normed.at[1])
    project_body(meta_ref, normed.at[0], normed.at[1], wq, wkv, q_ref, kv_ref)
    local_body(0, queue, meta_ref, width_ref, q_ref, kv_ref, acc_ref, stat_ref)


def project_body(meta_ref, own, other, wq, wkv, q_ref, kv_ref):
    for i, frame in enumerate((own, other)):
        kv_ref[i] = dot(frame[...], wkv[...]).astype(BF16)
        q_ref[i] = (dot(frame[...], wq[...]) * SCORE_FACTOR).astype(BF16)


def local_body(step, queue, meta_ref, width_ref, q_ref, kv_ref, acc_ref, stat_ref):
    place = meta_ref[2]
    group = kv_ref.shape[2] // 2
    for qi in range(2):
        here = place ^ qi
        slot = (here - step) & (queue - 1)
        reach = width_ref[slot]
        aside = 1 - 2 * (here & 1)
        allowed = (reach >= 0, within(slot, aside, reach, queue))
        for head in range(group // HEAD_DIM):
            lanes = slice(head * HEAD_DIM, (head + 1) * HEAD_DIM)
            value_lanes = slice(group + head * HEAD_DIM, group + (head + 1) * HEAD_DIM)
            query = q_ref[qi, :, lanes]
            scores = [scores_of(query, kv_ref[j, :, lanes]) for j in (qi, 1 - qi)]
            top = lane_max(scores, allowed)
            values = [kv_ref[j, :, value_lanes] for j in (qi, 1 - qi)]
            total, mixed = weigh(scores, allowed, top, values)
            acc_ref[qi, :, lanes] = mixed
            stat_ref[qi, :, head : head + 1] = top
            stat_ref[qi, :, 8 + head : 9 + head] = total


def halo_body(
    step, queue, meta_ref, width_ref, *refs
):
    sources, (q_ref, acc_in, stat_in, own_out, other_out, ks, vs) = refs[:-7], refs[-7:]
    group = ks.shape[2]
    place, behind = meta_ref[2], meta_ref[3]
    if step == 0:
        *frames, wkv = sources
        for i, frame in enumerate(frames):
            both = dot(frame[...], wkv[...])
            ks[i] = both[:, :group].astype(BF16)
            vs[i] = both[:, group:].astype(BF16)
    else:
        for i in range(4):
            ks[i] = sources[i // 2][i % 2, :, :group]
            vs[i] = sources[i // 2][i % 2, :, group:]
    for qi, out in enumerate((own_out, other_out)):
        here = place ^ qi
        slot = (here - step) & (queue - 1)
        reach = width_ref[slot]
        index, allowed = [], []
        for offset in (-2, 2, 2 * (here & 1) - 1):
            there = (here + offset) & (queue - 1)
            pick = jnp.int32(3)
            for j, known in enumerate((place ^ 2, place ^ 3, behind)):
                pick = jnp.where(there == known, j, pick)
            index.append(pick)
            allowed.append(within(slot, jnp.int32(offset), reach, queue))
        for head in range(ks.shape[2] // HEAD_DIM):
            lanes = slice(head * HEAD_DIM, (head + 1) * HEAD_DIM)
            query = q_ref[qi, :, lanes]
            scores = [scores_of(query, ks[j, :, lanes]) for j in index]
            before = stat_in[qi, :, head : head + 1]
            top = jnp.maximum(before, lane_max(scores, allowed))
            total, mixed = weigh(scores, allowed, top, [vs[j, :, lanes] for j in index])
            fade = jnp.exp2(before - top)
            total = total + fade * stat_in[qi, :, 8 + head : 9 + head]
            mixed = mixed + fade * acc_in[qi, :, lanes]
            out[:, lanes] = (mixed / total).astype(BF16)


def output_sums(mixed, weights):
    m_self, m_core, m_y, m_yx = mixed
    w_self, w_core, w_y0, w_y1, w_x0, w_x1 = weights
    wide = w_y0.shape[0]
    sums = dot(m_self[...], w_self[...]) + dot(m_core[...], w_core[...])
    sums += dot(m_y[:, :wide], w_y0[...]) + dot(m_y[:, wide:], w_y1[...])
    return sums + dot(m_yx[:, :wide], w_x0[...]) + dot(m_yx[:, wide:], w_x1[...])


def out_step_body(
    meta_ref,
    m_self, m_core, m_y, m_yx, *rest,
):
    lat_m, lat_t, fresh_m, fresh_t, mod_m, mod_t, vel_ref, next_ref, normed_ref = rest[12:]
    mixed = m_self, m_core, m_y, m_yx
    change = mod_m[CHANGE : CHANGE + 1, :]
    first = meta_ref[2] == 0
    fresh = (fresh_m[0], fresh_t[...])
    nexts = []
    for side, (lat, mod) in enumerate(((lat_m, mod_m), (lat_t, mod_t))):
        proj = output_sums(mixed, rest[6 * side : 6 * side + 6])
        state = lat[...].astype(F32)
        velocity = state + mod[GATE : GATE + 1, :] * proj
        updated = (state + change * velocity).astype(BF16)
        if side == 0:
            vel_ref[...] = velocity.astype(BF16)
        nexts.append(jnp.where(first, fresh[side].astype(F32), updated.astype(F32)))
    next_ref[...] = nexts[0].astype(BF16)
    normalize(
        nexts[0], nexts[1], lambda r: mod_m[r : r + 1, :], lambda r: mod_t[r : r + 1, :],
        3, meta_ref[0], normed_ref,
    )


def out_last_body(
    meta_ref,
    m_self, m_core, m_y, m_yx, *rest,
):
    latent, fresh, mod_m, vel_ref, upd_ref = rest[6:]
    proj = output_sums((m_self, m_core, m_y, m_yx), rest[:6])
    state = latent[...].astype(F32)
    velocity = state + mod_m[GATE + 3 : GATE + 4, :] * proj
    vel_ref[...] = velocity.astype(BF16)
    updated = state + mod_m[CHANGE + 1 : CHANGE + 2, :] * velocity
    leaves = meta_ref[2] == 1
    upd_ref[...] = jnp.where(leaves, fresh[0].astype(F32), updated).astype(BF16)


def join_body(meta_ref, latent, first, second, latent_ref, both_ref):
    latent_ref[...] = latent[...]
    both_ref[0] = first[...]
    both_ref[1] = second[...]


def tie(*arrays):
    return lax.optimization_barrier(arrays)


def per_device(
    latents, fresh_noise, level_index, window_width, w_mod, w_query, w_key, w_value, w_out
):
    queue = lax.axis_size("queue")
    place = lax.axis_index("queue")
    side = lax.axis_index("heads")
    core = place & 1
    chips = queue // 2

    def behind_of(f):
        chip = f >> 1
        return (((chip + 1 if chip & 1 else chip - 1) % chips) << 1) | (f & 1)

    chip = place >> 1
    behind = ((jnp.where(chip & 1 == 1, chip + 1, chip - 1) & (chips - 1)) << 1) | core
    crossed = ((place ^ behind) // chips) & 1
    meta = jnp.stack(
        [side, core, place, behind, crossed]
    ).astype(jnp.int32)

    rows, half = latents.shape[1:]
    group = half // 2
    wide = group - HEAD_DIM
    slots = range(queue)

    core_swap = [(f, f ^ 1) for f in slots]
    near = [(f, f ^ 2) for f in slots]
    far_ring = [
        (f * 2 + h, behind_of(f) * 2 + (h ^ (((f ^ behind_of(f)) // chips) & 1)))
        for f in slots
        for h in (0, 1)
    ]
    far_open = [(s, d if abs(s // 2 - d // 2) <= 2 else s) for s, d in far_ring]
    head_only = [(s, s ^ 1 if s < 2 else s) for s in range(2 * queue)]
    both = ("queue", "heads")

    def on_queue(x, perm):
        return lax.ppermute(x, "queue", perm)

    def on_sides(x):
        return lax.ppermute(x, "heads", [(0, 1), (1, 0)])

    def on_both(x, perm):
        return lax.ppermute(x, both, perm)

    def aside(to):
        return [(f * 2 + h, to(f) * 2 + 1 - h) for f in slots for h in (0, 1)]

    frame = jax.ShapeDtypeStruct((rows, 2 * half), BF16)
    half_frame = jax.ShapeDtypeStruct((rows, half), BF16)
    piece = jax.ShapeDtypeStruct((rows, group), BF16)
    pair = jax.ShapeDtypeStruct((2, rows, group), BF16)
    sums = jax.ShapeDtypeStruct((2, rows, group), F32)
    stats = jax.ShapeDtypeStruct((2, rows, HEAD_DIM), F32)

    def columns():
        return pl.BlockSpec((2 * half, group), lambda i, m, *_: (0, m[1]))

    def fresh_spec(step):
        return pl.BlockSpec((1, rows, half), lambda *_: (step, 0, 0))

    mine = latents[0]
    theirs = on_sides(mine)
    near_mine = on_queue(mine, near)
    far_mine = on_both(mine, far_open)

    (mod_mine,) = call(
        functools.partial(prepare_body, queue), [meta, level_index],
        [jnp.transpose(w_mod, (1, 0, 2))], [None],
        [jax.ShapeDtypeStruct((TABLE_ROWS, half), F32)],
        room=58 * 1024 * 1024,
    )
    mod_theirs = on_sides(mod_mine)
    w_query, w_pair, *send = call(
        pack_body, [meta], [w_query, w_key, w_value, w_out],
        [columns()] * 3 + [pl.BlockSpec((group, 2 * half), lambda i, m, *_: (m[1], 0))],
        [
            jax.ShapeDtypeStruct((2 * half, n), BF16) for n in (group, 2 * group)
        ] + [
            jax.ShapeDtypeStruct((n, 2 * half), BF16) for n in (wide, group - wide)
        ],
        room=58 * 1024 * 1024,
    )
    other_mine = on_queue(mine, core_swap)
    near_mine, far_mine, theirs, mod_mine, w_query, w_pair = tie(
        near_mine, far_mine, theirs, mod_mine, w_query, w_pair
    )
    other_theirs = on_queue(theirs, core_swap)

    def normed(pairs, jobs):
        args = [x for p in pairs for x in p] + [mod_mine, mod_theirs]
        return call(
            functools.partial(norm_body, jobs), [meta], args, [None] * len(args),
            [frame] * len(pairs),
        )

    def halo(step, sources, state):
        args = sources + state
        return call(
            functools.partial(halo_body, step, queue), [meta, window_width], args,
            [None] * len(args), [piece, piece],
            scratch=[pltpu.VMEM((4, rows, group), BF16)] * 2,
        )

    def exchanged(m_own, m_other):
        return [
            m_own, on_queue(m_other, core_swap), on_sides(m_own),
            on_both(m_other, aside(lambda f: f ^ 1)),
        ]

    def w_specs(flip):
        col = (lambda m: 1 - m[0]) if flip else (lambda m: m[0])
        return [
            pl.BlockSpec((group, half), lambda i, m, *_: (m[1], col(m))),
            pl.BlockSpec((group, half), lambda i, m, *_: (1 - m[1], col(m))),
        ] + [
            pl.BlockSpec((n, half), lambda i, m, *_: (0, col(m))) for n in (wide, group - wide)
        ] * 2

    near_theirs = on_sides(near_mine)
    far_theirs = on_both(theirs, far_open)
    state = call(
        functools.partial(first_local_body, queue), [meta, window_width],
        [mine, theirs, other_mine, other_theirs, mod_mine, mod_theirs, w_query, w_pair],
        [None] * 8, [pair, sums, stats],
        scratch=[
            pltpu.VMEM((2, rows, 2 * group), BF16), pltpu.VMEM((2, rows, 2 * half), BF16)
        ],
    )
    fresh_theirs = on_both(fresh_noise[0], head_only)
    near_theirs, far_theirs, fresh_theirs, *state = tie(
        near_theirs, far_theirs, fresh_theirs, *state
    )
    near_own, far_own = normed(
        [(near_mine, near_theirs), (far_mine, far_theirs)], [(1, False), (2, True)]
    )
    near_own, far_own, *send = tie(near_own, far_own, *send)
    far_weights = [on_both(send[0], aside(lambda f: f ^ chips)), on_sides(send[1])]
    near_own, far_own, *state = tie(near_own, far_own, *state)
    near_other = on_queue(near_own, core_swap)
    far_other = on_queue(far_own, core_swap)
    m_own, m_other = halo(0, [near_own, near_other, far_own, far_other, w_pair], state)
    mixed = exchanged(m_own, m_other)
    *far_weights, _, _ = tie(*far_weights, mixed[2], mixed[3])
    far_weights_other = [on_queue(w, core_swap) for w in far_weights]
    weights = [w_out, w_out, *far_weights, *far_weights_other]
    vel0, latent, own = call(
        out_step_body, [meta],
        mixed + weights * 2
        + [mine, theirs, fresh_noise, fresh_theirs, mod_mine, mod_theirs],
        [None] * 4 + w_specs(False) + w_specs(True) + [None, None, fresh_spec(0), None, None, None],
        [half_frame, half_frame, frame],
    )

    query, keyed = call(
        project_body, [meta], [own, on_queue(own, core_swap), w_query, w_pair], [None] * 4,
        [pair, jax.ShapeDtypeStruct((2, rows, 2 * group), BF16)],
    )
    near_keyed = on_queue(keyed, near)
    far_keyed = on_queue(keyed, [(f, behind_of(f)) for f in slots])
    sums0, stats0 = call(
        functools.partial(local_body, 1, queue), [meta, window_width], [query, keyed],
        [None] * 2, [sums, stats],
    )
    mixed = exchanged(*halo(1, [near_keyed, far_keyed], [query, sums0, stats0]))
    vel1, upd1 = call(
        out_last_body, [meta], mixed + weights + [latent, fresh_noise, mod_mine],
        [None] * 4 + w_specs(False) + [None, fresh_spec(1), None],
        [half_frame, half_frame],
    )
    latent = on_queue(upd1, [(f, (f - 2) % queue) for f in slots])
    vel1 = on_queue(vel1, [(f, (f - 1) % queue) for f in slots])
    latent, velocities = call(
        join_body, [meta], [latent, vel0, vel1], [None] * 3,
        [half_frame, jax.ShapeDtypeStruct((2, rows, half), BF16)],
    )
    return (latent[None], velocities[:, None])


def solution(mesh):
    in_specs = (
        P("queue", None, "heads"),
        P(None, None, "heads"),
        P(),
        P(),
        P(None, None, "heads"),
        P(None, "heads"),
        P(None, "heads"),
        P(None, "heads"),
        P("heads", None),
    )
    out_specs = (P("queue", None, "heads"), P(None, "queue", None, "heads"))
    return jax.shard_map(
        per_device, mesh=mesh, in_specs=in_specs, out_specs=out_specs, check_vma=False
    )
```
